32 devices in a mesh: groups: 2 (over x), gx: 16 (over z, y, core).
Axes of the slice: x: 2, y: 2, z: 4, core: 2. Of those that a mesh axis runs over, the one named last changes fastest.
Arguments:
- residual: bfloat16 [256, 18432], P('groups', 'gx'), parts along dimension 0, may hold values from -10.1 to 10.1
- norm_gain: float32 [18432], P('gx'), may hold values from 0.5 to 1.5
- w_query: bfloat16 [18432, 6144], P('gx'), may hold values from -0.046875 to 0.046875
- w_keyval: bfloat16 [18432, 512], P('gx'), may hold values from -0.09375 to 0.09375
- w_output: bfloat16 [6144, 18432], P(None, 'gx'), may hold values from -0.078125 to 0.078125
- key_cache: bfloat16 [256, 512, 256], P(('groups', 'gx')), parts along dimension 0, may hold values from -266 to 266
- value_cache: bfloat16 [256, 512, 256], P(('groups', 'gx')), parts along dimension 0, may hold values from -18 to 18
- lengths: int32 [256], P(('groups', 'gx')), parts along dimension 0, may hold values from 2 to 512, as said below
- positions: int32 [256], P(('groups', 'gx')), parts along dimension 0, may hold values from 2 to 767, as said below
Outputs:
- updated: float32 [256, 18432], P('groups', 'gx'), parts along dimension 0
- new_keyval: float32 [256, 512], P(('groups', 'gx')), parts along dimension 0
The draws below stay inside these ranges and needn't reach their ends.
There are 2 independent parts, one for each index of `groups`. The reference program is written for one: setup_inputs(seed, part) draws one part's arguments, and reference() takes and returns one part's arrays. A program takes and returns all parts, laid end to end along the dimension named above; an argument that names none is the same for every part. Nothing has to cross between parts.
Inputs may be any that keep to these rules, and one draw needn't show every extreme that they name: Slots 0 to lengths[b] - 1 of request b's cache are filled; some request has all 512 slots filled. `positions`: each request's position is its length plus 0 to 255; some request has position 767.
All inputs are finite; a program needn't handle non-finite values.
Results may differ from the reference program's by a relative error of at most 0.011.
Values may be sent and summed in bfloat16 or wider, within the bound.
No kernel may reach another device: no remote copies, remote signals or barrier semaphores. Data moves between devices by JAX's collectives and lax.ppermute only.
A program may use at most 128 MiB of HBM per device.

```python
import math
import jax
import jax.numpy as jnp
from jax import lax

D = 18432
HEADS = 24
HD = 256
CACHE = 512
ROWS_DEV = 8
QUERY_WIDTH = 6144
BATCH = 128
N_GX = 16


def draw_residual(key, part):
    key = jax.random.fold_in(key, 1)
    key_one, key_two, key_three = jax.random.split(key, 3)
    columns = jnp.arange(D, dtype=jnp.float32) / D
    column_scale = 0.2 * 10.0 ** columns * jax.random.uniform(key_two, (D,), jnp.float32, 0.7, 1.4)
    row_scale = jax.random.uniform(key_three, (BATCH, 1), jnp.float32, 0.6, 1.2)
    values = jax.random.truncated_normal(key_one, -3.0, 3.0, (BATCH, D), jnp.float32)
    return (values * column_scale[None, :] * row_scale).astype(jnp.bfloat16)


def draw_key_cache(key, part):
    key = jax.random.fold_in(key, 2)
    key_one = jax.random.fold_in(key, 0)
    values = 1.5 * jax.random.truncated_normal(key_one, -4.0, 4.0, (BATCH, CACHE, HD), jnp.float32)
    return values.astype(jnp.bfloat16)


def row_lengths(key):
    key_one, key_two, key_three = jax.random.split(key, 3)
    row_ids = jnp.arange(BATCH, dtype=jnp.int32)
    chosen_row = jax.random.randint(key_two, (), 0, BATCH, dtype=jnp.int32)
    filled = jax.random.randint(key_one, (BATCH,), 2, CACHE + 1, dtype=jnp.int32)
    filled = jnp.where(row_ids == chosen_row, CACHE, filled)
    offsets = jax.random.randint(key_three, (BATCH,), 0, 256, dtype=jnp.int32)
    offsets = jnp.where(row_ids == chosen_row, 255, offsets)
    return (filled, filled + offsets)


def draw_lengths(key, part):
    shared = row_lengths(key)
    return shared[0]


def draw_positions(key, part):
    shared = row_lengths(key)
    return shared[1]


def block_scale(rng, dims, cuts, smallest, top_value):
    loudness, own = 1.0, jax.random.fold_in(rng, 6)
    for dim, shards_of in cuts:
        steps = jnp.exp(jax.random.uniform(jax.random.fold_in(own, dim), (shards_of,), jnp.float32, smallest / len(cuts), top_value / len(cuts)))
        loudness = loudness * jnp.repeat(steps, dims[dim] // shards_of).reshape([-1 if axis == dim else 1 for axis in range(len(dims))])
    return loudness


def centred(stream_key, extent, scale, most, cuts=(), held_as=jnp.bfloat16):
    entries = jax.random.normal(stream_key, extent, jnp.float32) * scale
    if len(cuts) > 0:
        entries = block_scale(stream_key, extent, cuts, -0.22, 0.18) * entries
    return jnp.clip(entries, min=-most, max=most).astype(held_as)


def setup_inputs(seed: int = 0, part: int = 0) -> dict:
    key_list = jax.random.split(jax.random.key(seed), 10)
    own_keys = jax.random.split(jax.random.fold_in(key_list[9], part), 10)
    residual = draw_residual(jax.random.fold_in(jax.random.fold_in(key_list[9], part), 71), part)
    norm_gain = jnp.clip(1.0 + 0.1 * jax.random.normal(key_list[1], (D,), jnp.float32), 0.5, 1.5)
    w_query = centred(key_list[2], (D, QUERY_WIDTH), D ** -0.5, 0.046875, ((0, 16),))
    w_keyval = centred(key_list[3], (D, 2 * HD), (D // 4) ** -0.5, 0.09375, ((0, 16),))
    w_output = centred(key_list[4], (QUERY_WIDTH, D), QUERY_WIDTH ** -0.5, 0.078125, ((1, 16),))
    key_cache = draw_key_cache(jax.random.fold_in(jax.random.fold_in(key_list[9], part), 71), part)
    value_cache = centred(own_keys[6], (BATCH, CACHE, HD), 3.0, 18.0, ((0, 16),))
    lengths = draw_lengths(jax.random.fold_in(jax.random.fold_in(key_list[9], part), 71), part)
    positions = draw_positions(jax.random.fold_in(jax.random.fold_in(key_list[9], part), 71), part)
    return dict(residual=residual, norm_gain=norm_gain, w_query=w_query, w_keyval=w_keyval, w_output=w_output, key_cache=key_cache, value_cache=value_cache, lengths=lengths, positions=positions)


EPSILON = 1e-05

def rope_tables(position_rows):
    half_width = HD // 2
    inverse_freq = 10000.0 ** (-(jnp.arange(half_width, dtype=jnp.float32) * 2.0 / HD))
    angles = position_rows.astype(jnp.float32)[:, None] * inverse_freq[None, :]
    return (jnp.cos(angles), jnp.sin(angles))

def rotate_pairs(values, cosine, sine_part):
    half_width = values.shape[-1] // 2
    first = values[..., :half_width]
    second = values[..., half_width:]
    return jnp.concatenate([first * cosine - second * sine_part, second * cosine + first * sine_part], axis=-1)

def attend_rows(projected, key_block, value_block, length_rows, position_rows):
    row_total = projected.shape[0]
    query_width = projected.shape[1] - 2 * HD
    queries = projected[:, :query_width].reshape(row_total, query_width // HD, HD)
    new_key = projected[:, query_width:query_width + HD]
    new_value = projected[:, query_width + HD:]
    cosine, sine_part = rope_tables(position_rows)
    rotated_q = rotate_pairs(queries, cosine[:, None, :], sine_part[:, None, :]).astype(jnp.bfloat16)
    rotated_k = rotate_pairs(new_key, cosine, sine_part)
    new_keyval = jnp.concatenate([rotated_k, new_value], axis=1)
    key_rounded = rotated_k.astype(jnp.bfloat16)
    value_rounded = new_value.astype(jnp.bfloat16)
    scale_factor = 1.0 / math.sqrt(HD)
    scores = jnp.einsum('rhd,rkd->rhk', rotated_q.astype(jnp.float32), key_block.astype(jnp.float32)) * scale_factor
    own_score = jnp.einsum('rhd,rd->rh', rotated_q.astype(jnp.float32), key_rounded.astype(jnp.float32)) * scale_factor
    slot_ids = jnp.arange(key_block.shape[1], dtype=jnp.int32)
    valid = slot_ids[None, None, :] < length_rows.astype(jnp.int32)[:, None, None]
    masked = jnp.where(valid, scores, -jnp.inf)
    highest = jnp.maximum(lax.optimization_barrier(jnp.max(masked, axis=-1)), own_score)
    exps = jnp.exp(masked - highest[..., None])
    own_exp = jnp.exp(own_score - highest)
    denominator = lax.optimization_barrier(jnp.sum(exps, axis=-1)) + own_exp
    weights = (exps / denominator[..., None]).astype(jnp.bfloat16)
    own_weight = (own_exp / denominator).astype(jnp.bfloat16)
    attended = jnp.einsum('rhk,rkd->rhd', weights.astype(jnp.float32), value_block.astype(jnp.float32))
    attended = attended + own_weight.astype(jnp.float32)[..., None] * value_rounded.astype(jnp.float32)[:, None, :]
    return (attended.astype(jnp.bfloat16).reshape(row_total, query_width), new_keyval)

def reference(residual, norm_gain, w_query, w_keyval, w_output, key_cache, value_cache, lengths, positions):
    stream = residual.astype(jnp.float32)
    row_mean = lax.optimization_barrier(jnp.sum(stream, axis=1, keepdims=True)) / D
    row_square = lax.optimization_barrier(jnp.sum(stream * stream, axis=1, keepdims=True)) / D
    normed = ((stream - row_mean) * lax.rsqrt(row_square - row_mean * row_mean + EPSILON) * norm_gain[None, :]).astype(jnp.bfloat16)
    projected = jnp.concatenate([jnp.dot(normed, w_query, preferred_element_type=jnp.float32), jnp.dot(normed, w_keyval, preferred_element_type=jnp.float32)], axis=1)

    def blocked(array):
        return array.reshape((N_GX, ROWS_DEV) + array.shape[1:])

    def per_block(block_args):
        return attend_rows(block_args[0], block_args[1], block_args[2], block_args[3], block_args[4])
    attended, new_keyval = lax.map(per_block, (blocked(projected), blocked(key_cache), blocked(value_cache), blocked(lengths), blocked(positions)))
    attended = attended.reshape(BATCH, HEADS * HD)
    new_keyval = new_keyval.reshape(BATCH, 2 * HD)
    updated = stream + jnp.dot(attended, w_output, preferred_element_type=jnp.float32)
    return (updated, new_keyval)
```

```python
import functools
import math

import jax
import jax.numpy as jnp
from jax import lax
from jax.experimental import pallas as pl
from jax.experimental.pallas import tpu as pltpu
from jax.sharding import PartitionSpec as P

HD = 256
LANES = 128
BLOCK = 8
TILE = 512
EPSILON = 1e-05
VMEM = pl.BlockSpec(memory_space=pltpu.VMEM)
SMEM = pl.BlockSpec(memory_space=pltpu.SMEM)


def rope_tables(position_rows):
    half_width = HD // 2
    inverse_freq = 10000.0 ** (-(jnp.arange(half_width, dtype=jnp.float32) * 2.0 / HD))
    angles = position_rows.astype(jnp.float32)[:, None] * inverse_freq[None, :]
    return (jnp.cos(angles), jnp.sin(angles))


def exchange(value, mask, count):
    return lax.ppermute(value, "gx", [(i, i ^ mask) for i in range(count)])


def block_order(masks):
    order = [0]
    for mask in reversed(masks):
        order = order + [b | mask for b in order]
    return order


def struct(shape, dtype):
    return jax.ShapeDtypeStruct(shape, dtype)


def lane_ids(rows):
    return lax.broadcasted_iota(jnp.int32, (rows, LANES), 1)


def pack_stats(stats):
    high = stats.astype(jnp.bfloat16).astype(jnp.float32)
    middle = (stats - high).astype(jnp.bfloat16).astype(jnp.float32)
    low = stats - high - middle
    lane = lane_ids(stats.shape[0])
    return jnp.where(lane < 2, high, jnp.where(lane < 4, middle, low)).astype(jnp.bfloat16)


def unpack_stats(packed):
    parts = packed.astype(jnp.float32)
    mean = parts[:, 0:1] + parts[:, 2:3] + parts[:, 4:5]
    square = parts[:, 1:2] + parts[:, 3:4] + parts[:, 5:6]
    return jnp.where(lane_ids(parts.shape[0]) % 2 == 0, mean, square)


def project_kernel(order, me_ref, x_ref, gain_ref, wq_ref, wkv_ref, keep_ref, send_ref, stats_ref,
                   side_ref, rows_ref, lhs_ref):
    step = pl.program_id(0)
    total = x_ref.shape[0]
    half = total // 2
    me = me_ref[0]

    @pl.when(step == 0)
    def _():
        rows_ref[...] = x_ref[...].astype(jnp.float32)
        gain = gain_ref[...]
        high = gain.astype(jnp.bfloat16).astype(jnp.float32)
        low = gain - high
        row = lax.broadcasted_iota(jnp.int32, (16, gain.shape[1]), 0)
        lhs_ref[2 * total :, :] = jnp.where(
            row == 0, high, jnp.where(row == 1, low, 0.0)
        ).astype(jnp.bfloat16)
        lane = lane_ids(2 * BLOCK)
        side_ref[...] = jnp.zeros_like(side_ref)
        for pair in range(len(order) // 2):
            pieces = []
            for b in order[2 * pair : 2 * pair + 2]:
                start = pl.multiple_of((me ^ b) * BLOCK, BLOCK)
                pieces.append(rows_ref[pl.ds(start, BLOCK), :])
            x = jnp.concatenate(pieces, axis=0)
            mean = jnp.mean(x, axis=1, keepdims=True)
            square = jnp.mean(x * x, axis=1, keepdims=True)
            at = pair * 2 * BLOCK
            value = (x - mean) * gain
            rounded = value.astype(jnp.bfloat16)
            lhs_ref[at : at + 2 * BLOCK, :] = rounded
            lhs_ref[total + at : total + at + 2 * BLOCK, :] = (
                value - rounded.astype(jnp.float32)
            ).astype(jnp.bfloat16)
            stats_ref[at : at + 2 * BLOCK, :] = jnp.where(lane % 2 == 0, mean, square)

    def tile(weights):
        out = jnp.dot(lhs_ref[...], weights, preferred_element_type=jnp.float32)
        keep_ref[...] = out[:half] + out[total : total + half]
        send_ref[...] = (out[half:total] + out[total + half : 2 * total]).astype(jnp.bfloat16)
        gained = out[2 * total : 2 * total + 1] + out[2 * total + 1 : 2 * total + 2]
        for k in range(TILE // LANES):
            side_ref[pl.ds(step * (TILE // LANES) + k, 1), :] = gained[:, k * LANES : (k + 1) * LANES]

    @pl.when(step == 0)
    def _():
        tile(wkv_ref[...])

    @pl.when(step > 0)
    def _():
        tile(wq_ref[...])


def project(me, order, residual, gain, w_query, w_keyval):
    total, depth = residual.shape
    width = w_query.shape[1] + w_keyval.shape[1]
    half = total // 2
    chunks = width // LANES
    return pl.pallas_call(
        functools.partial(project_kernel, order),
        grid=(width // TILE,),
        in_specs=[
            SMEM,
            pl.BlockSpec((total, depth), lambda j: (0, 0)),
            pl.BlockSpec((1, depth), lambda j: (0, 0)),
            pl.BlockSpec((depth, TILE), lambda j: (0, jnp.maximum(j - 1, 0))),
            pl.BlockSpec((depth, TILE), lambda j: (0, 0)),
        ],
        out_specs=[
            pl.BlockSpec((half, TILE), lambda j: (0, j)),
            pl.BlockSpec((half, TILE), lambda j: (0, j)),
            pl.BlockSpec((total, LANES), lambda j: (0, 0)),
            pl.BlockSpec((chunks, LANES), lambda j: (0, 0)),
        ],
        out_shape=[
            struct((half, width), jnp.float32),
            struct((half, width), jnp.bfloat16),
            struct((total, LANES), jnp.float32),
            struct((chunks, LANES), jnp.float32),
        ],
        scratch_shapes=[
            pltpu.VMEM((total, depth), jnp.float32),
            pltpu.VMEM((2 * total + 16, depth), jnp.bfloat16),
        ],
        compiler_params=pltpu.CompilerParams(vmem_limit_bytes=24 * 2**20),
        name="project",
    )(me, residual, gain, w_query, w_keyval)


def first_kernel(keep_ref, recv_ref, stats_ref, other_stats_ref, side_ref, other_side_ref,
                 keep_a, keep_b, send_a, send_b, stats_a, stats_b, side_a, side_b):
    half, width = keep_ref.shape
    cut = width // 2
    chunks = cut // LANES
    half_a, quarter = half // 2, half // 4
    own = stats_ref[:half, :]
    other = other_stats_ref[...]
    merged = 0.5 * (own + other)
    shift = 0.5 * (own[:, 0:1] - other[:, 0:1])
    stats_a[...] = merged[:half_a]
    packed = pack_stats(merged)
    send_a[:, cut:] = packed[half_a:]
    for k in range(2):
        stats_b[k * quarter : (k + 1) * quarter, :] = merged[2 * k * quarter : (2 * k + 1) * quarter]
        send_b[k * quarter : (k + 1) * quarter, cut:] = packed[
            (2 * k + 1) * quarter : (2 * k + 2) * quarter
        ]
    for c in range(2 * chunks):
        columns = slice(c * LANES, (c + 1) * LANES)
        change = side_ref[c : c + 1, :] - other_side_ref[c : c + 1, :]
        total = keep_ref[:, columns] + recv_ref[:, columns].astype(jnp.float32) + shift * change
        if c < chunks:
            keep_a[:, columns] = total[:half_a]
            send_a[:, columns] = total[half_a:].astype(jnp.bfloat16)
        else:
            columns = slice((c - chunks) * LANES, (c - chunks + 1) * LANES)
            for k in range(2):
                at = slice(k * quarter, (k + 1) * quarter)
                keep_b[at, columns] = total[2 * k * quarter : (2 * k + 1) * quarter]
                send_b[at, columns] = total[
                    (2 * k + 1) * quarter : (2 * k + 2) * quarter
                ].astype(jnp.bfloat16)
    side_a[...] = side_ref[:chunks, :] + other_side_ref[:chunks, :]
    side_b[...] = side_ref[chunks:, :] + other_side_ref[chunks:, :]


def first_combine(keep, recv, stats, other_stats, side, other_side):
    half, width = keep.shape
    cut = width // 2
    rows = half // 2
    chunks = cut // LANES
    return pl.pallas_call(
        first_kernel,
        in_specs=[VMEM] * 6,
        out_specs=[VMEM] * 8,
        out_shape=[struct((rows, cut), jnp.float32)] * 2
        + [struct((rows, cut + LANES), jnp.bfloat16)] * 2
        + [struct((rows, LANES), jnp.float32)] * 2
        + [struct((chunks, LANES), jnp.float32)] * 2,
        compiler_params=pltpu.CompilerParams(vmem_limit_bytes=24 * 2**20),
        name="first_combine",
    )(keep, recv, stats, other_stats, side, other_side)


def middle_kernel(*refs):
    inputs, outputs = refs[:10], refs[10:]
    packed_output = len(outputs) == 4
    for half in range(2):
        keep, recv, stats, side, other_side = inputs[half::2]
        rows, cut = keep.shape
        low = rows // 2
        chunks = cut // LANES
        own = stats[...]
        other = unpack_stats(recv[:, cut:])
        merged = 0.5 * (own + other)
        shift = 0.5 * (own[:, 0:1] - other[:, 0:1])
        at = slice(0, low)
        if packed_output:
            keep_out, send_out, stats_out, side_out = outputs
            at = slice(half * low, (half + 1) * low)
            side_at = slice(half * chunks, (half + 1) * chunks)
        else:
            keep_out, send_out, stats_out, side_out = outputs[half::2]
            side_at = slice(0, chunks)
        stats_out[at, :] = merged[:low]
        for c in range(chunks):
            columns = slice(c * LANES, (c + 1) * LANES)
            change = side[c : c + 1, :] - other_side[c : c + 1, :]
            total = keep[:, columns] + recv[:, columns].astype(jnp.float32) + shift * change
            keep_out[at, columns] = total[:low]
            send_out[at, columns] = total[low:].astype(send_out.dtype)
        send_out[at, cut:] = pack_stats(merged[low:]).astype(send_out.dtype)
        side_out[side_at, :] = side[...] + other_side[...]


def middle_combine(keep, recv, stats, side, other_side):
    rows, cut = keep[0].shape
    low = rows // 2
    chunks = cut // LANES
    if low == BLOCK:
        out_shape = [
            struct((2 * low, cut), jnp.float32),
            struct((2 * low, cut + LANES), jnp.bfloat16),
            struct((2 * low, LANES), jnp.float32),
            struct((2 * chunks, LANES), jnp.float32),
        ]
    else:
        out_shape = (
            [struct((low, cut), jnp.float32)] * 2
            + [struct((low, cut + LANES), jnp.bfloat16)] * 2
            + [struct((low, LANES), jnp.float32)] * 2
            + [struct((chunks, LANES), jnp.float32)] * 2
        )
    return pl.pallas_call(
        middle_kernel,
        in_specs=[VMEM] * 10,
        out_specs=[VMEM] * len(out_shape),
        out_shape=out_shape,
        compiler_params=pltpu.CompilerParams(vmem_limit_bytes=24 * 2**20),
        name="middle_combine",
    )(*keep, *recv, *stats, *side, *other_side)


def attend_kernel(heads, length_ref, keep_ref, recv_ref, stats_ref, side_ref, other_side_ref,
                  cos_ref, sin_ref, key_ref, value_ref, attended_ref, keyval_ref, q_ref, out_ref):
    cut = keep_ref.shape[1]
    chunks = cut // LANES
    slots = key_ref.shape[1]
    own = stats_ref[...]
    other = unpack_stats(recv_ref[:, cut:])
    merged = 0.5 * (own + other)
    shift = 0.5 * (own[:, 0:1] - other[:, 0:1])
    mean, square = merged[:, 0:1], merged[:, 1:2]
    scale = lax.rsqrt(square - mean * mean + EPSILON)
    cosine, sine = cos_ref[...], sin_ref[...]
    upper = lax.broadcasted_iota(jnp.int32, (2 * BLOCK, LANES), 0) >= BLOCK
    new_key = new_value = None
    for c in range(0, chunks, 2):
        pair = []
        for d in (c, c + 1):
            columns = slice(d * LANES, (d + 1) * LANES)
            change = jnp.where(
                upper,
                side_ref[chunks + d : chunks + d + 1, :] - other_side_ref[chunks + d : chunks + d + 1, :],
                side_ref[d : d + 1, :] - other_side_ref[d : d + 1, :],
            )
            total = keep_ref[:, columns] + recv_ref[:, columns].astype(jnp.float32) + shift * change
            pair.append(total * scale)
        for half in range(2):
            u1, u2 = (v[half * BLOCK : (half + 1) * BLOCK] for v in pair)
            number = half * (chunks // 2) + c // 2 - 2
            if number == -1:
                new_value = jnp.concatenate([u1, u2], axis=1)
                continue
            turned = jnp.concatenate([u1 * cosine - u2 * sine, u2 * cosine + u1 * sine], axis=1)
            if number == -2:
                new_key = turned
            else:
                for k in range(2):
                    q_ref[k, number * BLOCK : (number + 1) * BLOCK, :] = turned[
                        :, k * LANES : (k + 1) * LANES
                    ]
    keyval_ref[:, :HD] = new_key
    keyval_ref[:, HD:] = new_value
    factor = 1.0 / math.sqrt(HD)
    slot = lax.broadcasted_iota(jnp.int32, (heads, slots), 1)
    for r in range(BLOCK):
        queries = jnp.concatenate(
            [q_ref.at[k][pl.ds(r, heads, stride=BLOCK), :] for k in range(2)], axis=1
        ).astype(jnp.bfloat16)
        key_row = new_key[r : r + 1].astype(jnp.bfloat16).astype(jnp.float32)
        value_row = new_value[r : r + 1].astype(jnp.bfloat16).astype(jnp.float32)
        scores = (
            lax.dot_general(
                queries, key_ref[r], (((1,), (1,)), ((), ())), preferred_element_type=jnp.float32
            )
            * factor
        )
        own_score = (
            jnp.sum(queries.astype(jnp.float32) * key_row, axis=1, keepdims=True) * factor
        )
        masked = jnp.where(slot < length_ref[r], scores, -jnp.inf)
        highest = jnp.maximum(jnp.max(masked, axis=1, keepdims=True), own_score)
        exps = jnp.exp(masked - highest)
        own_exp = jnp.exp(own_score - highest)
        denominator = jnp.sum(exps, axis=1, keepdims=True) + own_exp
        weights = (exps / denominator).astype(jnp.bfloat16)
        own_weight = (own_exp / denominator).astype(jnp.bfloat16).astype(jnp.float32)
        mixed = jnp.dot(weights, value_ref[r], preferred_element_type=jnp.float32)
        mixed = mixed + own_weight * value_row
        for k in range(2):
            out_ref.at[k][pl.ds(r, heads, stride=BLOCK), :] = mixed[:, k * LANES : (k + 1) * LANES]
    for h in range(heads // 2):
        upper_head = h + heads // 2
        for k in range(2):
            at = h * HD + k * LANES
            attended_ref[:, at : at + LANES] = jnp.concatenate(
                [out_ref[k, g * BLOCK : (g + 1) * BLOCK, :] for g in (h, upper_head)], axis=0
            ).astype(jnp.bfloat16)


def attend(lengths, keep, recv, stats, side, other_side, tables, key_cache, value_cache, heads):
    return pl.pallas_call(
        functools.partial(attend_kernel, heads),
        in_specs=[SMEM] + [VMEM] * 9,
        out_specs=[VMEM] * 2,
        out_shape=[
            struct((2 * BLOCK, heads * HD // 2), jnp.bfloat16),
            struct((BLOCK, 2 * HD), jnp.float32),
        ],
        scratch_shapes=[
            pltpu.VMEM((2, heads * BLOCK, LANES), jnp.float32),
            pltpu.VMEM((2, heads * BLOCK, LANES), jnp.float32),
        ],
        compiler_params=pltpu.CompilerParams(vmem_limit_bytes=24 * 2**20),
        name="attend",
    )(lengths, keep, recv, stats, side, other_side, *tables, key_cache, value_cache)


def output_kernel(order, me_ref, a_own, a_other, b_own, b_other, x_ref, w_ref, out_ref, lhs_ref,
                  acc_ref, rows_ref):
    step = pl.program_id(0)
    total = x_ref.shape[0]
    half = total // 2
    quarter = half // 4
    cut = a_own.shape[1]
    me = me_ref[0]

    @pl.when(step == 0)
    def _():
        lhs_ref[:half, :cut] = a_own[...]
        lhs_ref[half:, :cut] = a_other[...]
        for side, b in enumerate((b_own, b_other)):
            for k, source in enumerate((0, 2, 1, 3)):
                at = side * half + k * quarter
                lhs_ref[at : at + quarter, cut:] = b[source * quarter : (source + 1) * quarter, :]
        acc_ref[...] = jnp.zeros_like(acc_ref)
        rows_ref[...] = x_ref[...].astype(jnp.float32)

    depth = w_ref.shape[0]
    columns = pl.ds(pl.multiple_of(step * depth, depth), depth)
    acc_ref[...] += jnp.dot(lhs_ref[:, columns], w_ref[...], preferred_element_type=jnp.float32)

    @pl.when(step == pl.num_programs(0) - 1)
    def _():
        for p, b in enumerate(order):
            at = pl.ds(pl.multiple_of((me ^ b) * BLOCK, BLOCK), BLOCK)
            out_ref[at, :] = rows_ref[at, :] + acc_ref[p * BLOCK : (p + 1) * BLOCK, :]


def output(me, order, pieces, residual, w_output):
    total, width = residual.shape
    depth = w_output.shape[0]
    half, cut = pieces[0].shape
    steps = 6
    whole = lambda j: (0, 0)
    return pl.pallas_call(
        functools.partial(output_kernel, order),
        grid=(steps,),
        in_specs=[SMEM]
        + [pl.BlockSpec((half, cut), whole)] * 4
        + [
            pl.BlockSpec((total, width), whole),
            pl.BlockSpec((depth // steps, width), lambda j: (j, 0)),
        ],
        out_specs=pl.BlockSpec((total, width), whole),
        out_shape=struct((total, width), jnp.float32),
        scratch_shapes=[
            pltpu.VMEM((total, depth), jnp.bfloat16),
            pltpu.VMEM((total, width), jnp.float32),
            pltpu.VMEM((total, width), jnp.float32),
        ],
        compiler_params=pltpu.CompilerParams(vmem_limit_bytes=30 * 2**20),
        name="output",
    )(me, *pieces, residual, w_output)


def local(
    residual, norm_gain, w_query, w_keyval, w_output, key_cache, value_cache, lengths, positions
):
    count = lax.axis_size("gx")
    me = lax.axis_index("gx").astype(jnp.int32).reshape(1)
    heads = w_query.shape[1] // HD
    masks = [1 << k for k in range(count.bit_length() - 1)]
    paths = (masks, [masks[0], masks[2], masks[1]] + masks[3:])
    order = block_order(masks)
    half = count * BLOCK // 2
    tables = rope_tables(positions)

    keep, send, stats, side = project(
        me, order, residual, norm_gain[None, :], w_query, w_keyval
    )
    recv = exchange(send, masks[0], count)
    other_stats = exchange(stats[half:], masks[0], count)
    other_side = exchange(side, masks[0], count)
    state = first_combine(keep, recv, stats, other_stats, side, other_side)
    for level in range(1, len(masks) - 1):
        keep, send, stats, side = (state[k : k + 2] for k in range(0, 8, 2))
        recv = [exchange(v, path[level], count) for v, path in zip(send, paths)]
        other_side = [exchange(v, path[level], count) for v, path in zip(side, paths)]
        state = middle_combine(keep, recv, stats, side, other_side)
    keep, send, stats, side = state
    recv = exchange(send, masks[-1], count)
    other_side = exchange(side, masks[-1], count)
    attended, new_keyval = attend(
        lengths, keep, recv, stats, side, other_side, tables, key_cache, value_cache, heads
    )

    far = exchange(attended, masks[-1], count)
    pieces = []
    for path, rows in zip(paths, (slice(0, BLOCK), slice(BLOCK, 2 * BLOCK))):
        part = jnp.concatenate([attended[rows], far[rows]])
        for mask in path[-2:0:-1]:
            part = jnp.concatenate([part, exchange(part, mask, count)])
        pieces += [part, exchange(part, masks[0], count)]
    updated = output(me, order, pieces, residual, w_output)
    return (updated, new_keyval)


def solution(mesh):
    in_specs = (
        P("groups", "gx"),
        P("gx"),
        P("gx", None),
        P("gx", None),
        P(None, "gx"),
        P(("groups", "gx"), None, None),
        P(("groups", "gx"), None, None),
        P(("groups", "gx")),
        P(("groups", "gx")),
    )
    out_specs = (P("groups", "gx"), P(("groups", "gx"), None))
    return jax.shard_map(local, mesh=mesh, in_specs=in_specs, out_specs=out_specs, check_vma=False)
```

```python
import functools
import math

import jax
import jax.numpy as jnp
from jax import lax
from jax.experimental import pallas as pl
from jax.experimental.pallas import tpu as pltpu
from jax.sharding import PartitionSpec as P

HD = 256
LANES = 128
BLOCK = 8
TILE = 512
SIDE = 32
AHEAD = 3
PACE = 2
QUAD = 4
EPSILON = 1e-05
VMEM = pl.BlockSpec(memory_space=pltpu.VMEM)
SMEM = pl.BlockSpec(memory_space=pltpu.SMEM)


def rope_tables(position_rows):
    half_width = HD // 2
    inverse_freq = 10000.0 ** (-(jnp.arange(half_width, dtype=jnp.float32) * 2.0 / HD))
    angles = position_rows.astype(jnp.float32)[:, None] * inverse_freq[None, :]
    return (jnp.cos(angles), jnp.sin(angles))


def exchange(value, mask, count):
    return lax.ppermute(value, "gx", [(i, i ^ mask) for i in range(count)])


def in_hbm(value):
    return pltpu.with_memory_space_constraint(value, pltpu.HBM)


def struct(shape, dtype):
    return jax.ShapeDtypeStruct(shape, dtype)


def lane_ids(rows):
    return lax.broadcasted_iota(jnp.int32, (rows, LANES), 1)


def pack_stats(stats):
    high = stats.astype(jnp.bfloat16).astype(jnp.float32)
    middle = (stats - high).astype(jnp.bfloat16).astype(jnp.float32)
    low = stats - high - middle
    lane = lane_ids(stats.shape[0])
    return jnp.where(lane < 2, high, jnp.where(lane < 4, middle, low)).astype(jnp.bfloat16)


def unpack_stats(packed):
    parts = packed.astype(jnp.float32)
    mean = parts[:, 0:1] + parts[:, 2:3] + parts[:, 4:5]
    square = parts[:, 1:2] + parts[:, 3:4] + parts[:, 5:6]
    return jnp.where(lane_ids(parts.shape[0]) % 2 == 0, mean, square)


def pack_side(side):
    pieces = []
    for start in range(0, SIDE, BLOCK):
        pieces.append(
            jnp.concatenate(
                [side[start : start + BLOCK], side[SIDE + start : SIDE + start + BLOCK]], axis=0
            )
        )
    return jnp.concatenate(pieces, axis=1)


def folded_row(packed, c):
    part = packed[:, c // BLOCK * LANES : (c // BLOCK + 1) * LANES]
    k = c % BLOCK
    upper = lax.broadcasted_iota(jnp.int32, (2 * BLOCK, LANES), 0) >= BLOCK
    return jnp.where(upper, part[BLOCK + k : BLOCK + k + 1], part[k : k + 1])


def merge_stats(parts):
    merged = sum(parts[1:], parts[0]) * (1.0 / len(parts))
    return merged, [p[:, 0:1] - merged[:, 0:1] for p in parts]


def project_kernel(order, me_ref, x_hbm, gain_hbm, wq_hbm, wkv_hbm, keep_ref, send_ref, stats_ref,
                   extra_ref, x_ref, gain_ref, rows_ref, lhs_ref, w_ref, in_sem, w_sem):
    total = x_ref.shape[0]
    half = total // 2
    me = me_ref[0]
    tiles = w_ref.shape[0]
    x_copy = pltpu.make_async_copy(x_hbm, x_ref, in_sem.at[0])
    gain_copy = pltpu.make_async_copy(gain_hbm, gain_ref, in_sem.at[1])
    x_copy.start()
    gain_copy.start()
    copies = []
    for t in range(tiles):
        source = wkv_hbm if t == 0 else wq_hbm.at[:, (t - 1) * TILE : t * TILE]
        copies.append(pltpu.make_async_copy(source, w_ref.at[t], w_sem.at[t]))
    x_copy.wait()
    gain_copy.wait()
    started = min(AHEAD, tiles)
    for t in range(started):
        copies[t].start()
    rows_ref[...] = x_ref[...].astype(jnp.float32)
    gain = gain_ref[...].reshape(1, gain_ref.shape[0])
    high = gain.astype(jnp.bfloat16).astype(jnp.float32)
    low = gain - high
    row = lax.broadcasted_iota(jnp.int32, (16, gain.shape[1]), 0)
    lhs_ref[total:, :] = jnp.where(
        row == 0, high, jnp.where(row == 1, low, 0.0)
    ).astype(jnp.bfloat16)
    lane = lane_ids(2 * BLOCK)
    extra_ref[half:, :] = jnp.zeros((2 * SIDE, LANES), jnp.float32)
    for pair in range(len(order) // 2):
        pieces = []
        for b in order[2 * pair : 2 * pair + 2]:
            start = pl.multiple_of((me ^ b) * BLOCK, BLOCK)
            pieces.append(rows_ref[pl.ds(start, BLOCK), :])
        x = jnp.concatenate(pieces, axis=0)
        mean = jnp.mean(x, axis=1, keepdims=True)
        square = jnp.mean(x * x, axis=1, keepdims=True)
        at = pair * 2 * BLOCK
        lhs_ref[at : at + 2 * BLOCK, :] = ((x - mean) * gain).astype(jnp.bfloat16)
        if started < tiles - 1 and pair % PACE == PACE - 1:
            copies[started].start()
            started += 1
        stats = jnp.where(lane % 2 == 0, mean, square)
        if at < half:
            stats_ref[at : at + 2 * BLOCK, :] = stats
        else:
            extra_ref[at - half : at - half + 2 * BLOCK, :] = stats

    chunks = tiles * (TILE // LANES) // 2
    for t in range(tiles):
        while started < min(tiles, t + AHEAD + 4):
            copies[started].start()
            started += 1
        copies[t].wait()
        out = jnp.dot(lhs_ref[...], w_ref[t], preferred_element_type=jnp.float32)
        columns = slice(t * TILE, (t + 1) * TILE)
        keep_ref[:, columns] = out[:half]
        send_ref[:, columns] = out[half:total].astype(jnp.bfloat16)
        gained = out[total : total + 1] + out[total + 1 : total + 2]
        for k in range(TILE // LANES):
            c = t * (TILE // LANES) + k
            at = half + c if c < chunks else half + SIDE + c - chunks
            extra_ref[at : at + 1, :] = gained[:, k * LANES : (k + 1) * LANES]


def project(me, order, residual, gain, w_query, w_keyval):
    total, depth = residual.shape
    width = w_query.shape[1] + w_keyval.shape[1]
    half = total // 2
    tiles = width // TILE
    return pl.pallas_call(
        functools.partial(project_kernel, order),
        in_specs=[SMEM] + [pl.BlockSpec(memory_space=pltpu.HBM)] * 4,
        out_specs=[VMEM] * 4,
        out_shape=[
            struct((half, width), jnp.float32),
            struct((half, width), jnp.bfloat16),
            struct((half, LANES), jnp.float32),
            struct((half + 2 * SIDE, LANES), jnp.float32),
        ],
        scratch_shapes=[
            pltpu.VMEM((total, depth), jnp.bfloat16),
            pltpu.VMEM((depth,), jnp.float32),
            pltpu.VMEM((total, depth), jnp.float32),
            pltpu.VMEM((total + 16, depth), jnp.bfloat16),
            pltpu.VMEM((tiles, depth, TILE), jnp.bfloat16),
            pltpu.SemaphoreType.DMA((2,)),
            pltpu.SemaphoreType.DMA((tiles,)),
        ],
        compiler_params=pltpu.CompilerParams(vmem_limit_bytes=24 * 2**20),
        name="project",
    )(me, *(in_hbm(v) for v in (residual, gain, w_query, w_keyval)))


def first_kernel(keep_ref, recv_ref, stats_ref, extra_ref, other_ref,
                 own_ref, far_ref, own_stats, far_stats, side_ref, *send_refs):
    half, width = keep_ref.shape
    cut = width // 2
    chunks = cut // LANES
    early, late = send_refs[: QUAD - 1], send_refs[QUAD - 1 :]
    own = stats_ref[...]
    other = other_ref[:half, :]
    merged = 0.5 * (own + other)
    shift = 0.5 * (own[:, 0:1] - other[:, 0:1])
    side = extra_ref[half:, :] + other_ref[half:, :]
    change = extra_ref[half:, :] - other_ref[half:, :]
    side_ref[...] = side
    packed_side = pack_side(side).astype(jnp.bfloat16)
    fold = 2 * BLOCK

    def target(k):
        group, q = divmod(k, QUAD)
        return group, q, slice((group - 1) * fold, group * fold)

    for k in range(half // BLOCK):
        group, q, at = target(k)
        stats = merged[k * BLOCK : (k + 1) * BLOCK]
        stats = jnp.concatenate([stats, stats], axis=0)
        if q == 0:
            if group == 0:
                own_stats[...] = stats
            else:
                far_stats[at, :] = stats
        elif group == 0:
            late[q - 1][:, cut:] = pack_stats(stats)
        else:
            early[q - 1][at, cut : cut + LANES] = pack_stats(stats)
            early[q - 1][at, cut + LANES :] = packed_side
    for c in range(chunks):
        columns = slice(c * LANES, (c + 1) * LANES)
        totals = []
        for n in range(2):
            source = slice(n * cut + c * LANES, n * cut + (c + 1) * LANES)
            row = n * SIDE + c
            totals.append(
                keep_ref[:, source]
                + recv_ref[:, source].astype(jnp.float32)
                + shift * change[row : row + 1]
            )
        for k in range(half // BLOCK):
            group, q, at = target(k)
            value = jnp.concatenate([t[k * BLOCK : (k + 1) * BLOCK] for t in totals], axis=0)
            if q == 0:
                if group == 0:
                    own_ref[:, columns] = value
                else:
                    far_ref[at, columns] = value
            elif group == 0:
                late[q - 1][:, columns] = value.astype(jnp.bfloat16)
            else:
                early[q - 1][at, columns] = value.astype(jnp.bfloat16)


def first_combine(keep, recv, stats, extra, other):
    half, width = keep.shape
    cut = width // 2
    fold = 2 * BLOCK
    groups = half // (QUAD * BLOCK)
    far = (groups - 1) * fold
    return pl.pallas_call(
        first_kernel,
        in_specs=[VMEM] * 5,
        out_specs=[VMEM] * (5 + 2 * (QUAD - 1)),
        out_shape=[
            struct((fold, cut), jnp.float32),
            struct((far, cut), jnp.float32),
            struct((fold, LANES), jnp.float32),
            struct((far, LANES), jnp.float32),
            struct((2 * SIDE, LANES), jnp.float32),
        ]
        + [struct((far, cut + LANES + SIDE // BLOCK * LANES), jnp.bfloat16)] * (QUAD - 1)
        + [struct((fold, cut + LANES), jnp.bfloat16)] * (QUAD - 1),
        compiler_params=pltpu.CompilerParams(vmem_limit_bytes=16 * 2**20),
        name="first_combine",
    )(keep, recv, stats, extra, other)


def far_kernel(far_ref, stats_ref, side_ref, *refs):
    recv, outs = refs[: QUAD - 1], refs[QUAD:]
    cut = far_ref.shape[1]
    fold = 2 * BLOCK
    packed = [r[:fold, cut + LANES :].astype(jnp.float32) for r in recv]
    packed = [pack_side(side_ref[...])] + packed
    summed = sum(packed[1:], packed[0])
    outs[0][...] = summed
    for g, out in enumerate(outs[1:]):
        at = slice(g * fold, (g + 1) * fold)
        parts = [stats_ref[at, :]] + [unpack_stats(r[at, cut : cut + LANES]) for r in recv]
        merged, shifts = merge_stats(parts)
        out[:, cut : cut + LANES] = pack_stats(merged)
        out[:, cut + LANES :] = summed.astype(jnp.bfloat16)
        for c in range(cut // LANES):
            columns = slice(c * LANES, (c + 1) * LANES)
            total = far_ref[at, columns]
            for r in recv:
                total = total + r[at, columns].astype(jnp.float32)
            for shift, side in zip(shifts, packed):
                total = total + shift * folded_row(side, c)
            out[:, columns] = total.astype(jnp.bfloat16)


def far_combine(far, stats, side, recv, after):
    cut = far.shape[1]
    fold = 2 * BLOCK
    groups = far.shape[0] // fold
    side_columns = SIDE // BLOCK * LANES
    return pl.pallas_call(
        far_kernel,
        in_specs=[VMEM] * (3 + QUAD - 1) + [pl.BlockSpec(memory_space=pl.ANY)],
        out_specs=[VMEM] * (1 + groups),
        out_shape=[struct((fold, side_columns), jnp.float32)]
        + [struct((fold, cut + LANES + side_columns), jnp.bfloat16)] * groups,
        compiler_params=pltpu.CompilerParams(vmem_limit_bytes=16 * 2**20),
        name="far_combine",
    )(far, stats, side, *recv, after)


def two_part_dot(left, right, dims):
    rows = left.shape[0]
    high = left.astype(jnp.bfloat16)
    low = (left - high.astype(jnp.float32)).astype(jnp.bfloat16)
    both = jnp.concatenate([high.astype(jnp.float32), low.astype(jnp.float32)], axis=0)
    out = lax.dot_general(
        both.astype(jnp.bfloat16), right, dims, preferred_element_type=jnp.float32
    )
    return out[:rows] + out[rows:]


def attend_kernel(heads, length_ref, own_ref, stats_ref, side_ref, summed_ref, cos_ref, sin_ref,
                  key_ref, value_ref, *refs):
    early, late = refs[: QUAD - 1], refs[QUAD - 1 : 2 * QUAD - 2]
    far, (attended_ref, keyval_ref, q_ref, out_ref) = refs[2 * QUAD - 2 : -4], refs[-4:]
    cut = own_ref.shape[1]
    chunks = cut // LANES
    slots = key_ref.shape[1]
    fold = 2 * BLOCK
    parts = [stats_ref[...]] + [unpack_stats(r[:, cut:]) for r in late]
    merged, near_shifts = merge_stats(parts)
    packed = [pack_side(side_ref[...])]
    packed += [r[:fold, cut + LANES :].astype(jnp.float32) for r in early]
    parts = [merged] + [unpack_stats(r[:, cut : cut + LANES]) for r in far]
    merged, far_shifts = merge_stats(parts)
    packed += [summed_ref[...]] + [r[:, cut + LANES :].astype(jnp.float32) for r in far]
    shifts = near_shifts + far_shifts
    mean, square = merged[:, 0:1], merged[:, 1:2]
    scale = lax.rsqrt(square - mean * mean + EPSILON)
    cosine, sine = cos_ref[...], sin_ref[...]
    new_key = new_value = None
    for c in range(0, chunks, 2):
        pair = []
        for d in (c, c + 1):
            columns = slice(d * LANES, (d + 1) * LANES)
            total = own_ref[:, columns]
            for r in (*late, *far):
                total = total + r[:, columns].astype(jnp.float32)
            for shift, side in zip(shifts, packed):
                total = total + shift * folded_row(side, d)
            pair.append(total * scale)
        for half in range(2):
            u1, u2 = (v[half * BLOCK : (half + 1) * BLOCK] for v in pair)
            number = half * (chunks // 2) + c // 2 - 2
            if number == -1:
                new_value = jnp.concatenate([u1, u2], axis=1)
                continue
            turned = (u1 * cosine - u2 * sine, u2 * cosine + u1 * sine)
            if number == -2:
                new_key = jnp.concatenate(turned, axis=1)
            else:
                for k in range(2):
                    q_ref[k, number * BLOCK : (number + 1) * BLOCK, :] = turned[k]
    keyval_ref[:, :HD] = new_key
    keyval_ref[:, HD:] = new_value
    factor = 1.0 / math.sqrt(HD)
    slot = lax.broadcasted_iota(jnp.int32, (heads, slots), 1)
    key_rounded = new_key.astype(jnp.bfloat16).astype(jnp.float32)
    value_rounded = new_value.astype(jnp.bfloat16).astype(jnp.float32)
    requests = range(BLOCK)
    queries = [
        jnp.concatenate(
            [q_ref.at[k][pl.ds(r, heads, stride=BLOCK), :] for k in range(2)], axis=1
        )
        for r in requests
    ]
    scores = [
        two_part_dot(queries[r], key_ref[r], (((1,), (1,)), ((), ()))) for r in requests
    ]
    own_scores = [
        jnp.sum(queries[r] * key_rounded[r : r + 1], axis=1, keepdims=True)
        * factor
        for r in requests
    ]
    masked = [jnp.where(slot < length_ref[r], scores[r] * factor, -jnp.inf) for r in requests]
    highest = [
        jnp.maximum(jnp.max(masked[r], axis=1, keepdims=True), own_scores[r]) for r in requests
    ]
    exps = [jnp.exp(masked[r] - highest[r]) for r in requests]
    own_exps = [jnp.exp(own_scores[r] - highest[r]) for r in requests]
    inverse = [
        1.0 / (jnp.sum(exps[r], axis=1, keepdims=True) + own_exps[r]) for r in requests
    ]
    mixed = [
        two_part_dot(exps[r], value_ref[r], (((1,), (0,)), ((), ()))) * inverse[r] for r in requests
    ]
    for r in requests:
        own_weight = own_exps[r] * inverse[r]
        result = mixed[r] + own_weight * value_rounded[r : r + 1]
        for k in range(2):
            out_ref.at[k][pl.ds(r, heads, stride=BLOCK), :] = result[:, k * LANES : (k + 1) * LANES]
    for h in range(heads // 2):
        upper_head = h + heads // 2
        for k in range(2):
            at = h * HD + k * LANES
            attended_ref[:, at : at + LANES] = jnp.concatenate(
                [out_ref[k, g * BLOCK : (g + 1) * BLOCK, :] for g in (h, upper_head)], axis=0
            ).astype(jnp.bfloat16)


def attend(lengths, own, stats, side, summed, tables, key_cache, value_cache, early, late, far,
           heads):
    return pl.pallas_call(
        functools.partial(attend_kernel, heads),
        in_specs=[SMEM] + [VMEM] * (8 + len(early) + len(late) + len(far)),
        out_specs=[VMEM] * 2,
        out_shape=[
            struct((2 * BLOCK, heads * HD // 2), jnp.bfloat16),
            struct((BLOCK, 2 * HD), jnp.float32),
        ],
        scratch_shapes=[
            pltpu.VMEM((2, heads * BLOCK, LANES), jnp.float32),
            pltpu.VMEM((2, heads * BLOCK, LANES), jnp.float32),
        ],
        compiler_params=pltpu.CompilerParams(vmem_limit_bytes=24 * 2**20),
        name="attend",
    )(
        lengths, own, stats, side, summed, *tables, key_cache, value_cache, *early, *late, *far
    )


def load_kernel(w_hbm, after_ref, out_ref, token_ref, sems):
    parts = sems.shape[0]
    rows = w_hbm.shape[0] // parts
    copies = [
        pltpu.make_async_copy(
            w_hbm.at[k * rows : (k + 1) * rows, :], out_ref.at[k * rows : (k + 1) * rows, :], sems.at[k]
        )
        for k in range(parts)
    ]
    for copy in copies:
        copy.start()
    for copy in copies:
        copy.wait()
    token_ref[...] = jnp.zeros_like(token_ref)


def load(w_output, after):
    return pl.pallas_call(
        load_kernel,
        in_specs=[pl.BlockSpec(memory_space=pltpu.HBM), pl.BlockSpec(memory_space=pl.ANY)],
        out_specs=[VMEM] * 2,
        out_shape=[struct(w_output.shape, w_output.dtype), struct((BLOCK, LANES), jnp.float32)],
        scratch_shapes=[pltpu.SemaphoreType.DMA((8,))],
        compiler_params=pltpu.CompilerParams(vmem_limit_bytes=16 * 2**20),
        cost_estimate=pl.CostEstimate(
            flops=0, bytes_accessed=2 * w_output.size, transcendentals=0
        ),
        name="load",
    )(in_hbm(w_output), after)


def unfold(lhs_ref, pieces):
    cut = pieces[0].shape[1]
    for k in range(0, len(pieces), 2):
        pair = [p[...].astype(jnp.float32) for p in pieces[k : k + 2]]
        at = slice(k * BLOCK, (k + 2) * BLOCK)
        lhs_ref[at, :cut] = jnp.concatenate([p[:BLOCK] for p in pair], axis=0).astype(jnp.bfloat16)
        lhs_ref[at, cut:] = jnp.concatenate([p[BLOCK:] for p in pair], axis=0).astype(jnp.bfloat16)


def near_output_kernel(w_ref, *refs):
    pieces, (out_ref, lhs_ref) = refs[:-2], refs[-2:]
    unfold(lhs_ref, pieces)
    out_ref[...] = jnp.dot(lhs_ref[...], w_ref[...], preferred_element_type=jnp.float32)


def near_output(pieces, w_output):
    rows = len(pieces) * BLOCK
    depth, width = w_output.shape
    return pl.pallas_call(
        near_output_kernel,
        in_specs=[VMEM] * (1 + len(pieces)),
        out_specs=VMEM,
        out_shape=struct((rows, width), jnp.float32),
        scratch_shapes=[pltpu.VMEM((rows, depth), jnp.bfloat16)],
        compiler_params=pltpu.CompilerParams(vmem_limit_bytes=24 * 2**20),
        cost_estimate=pl.CostEstimate(
            flops=2 * rows * depth * width, bytes_accessed=4 * 2**20, transcendentals=0
        ),
        name="near_output",
    )(w_output, *pieces)


def far_output_kernel(near_order, far_order, me_ref, near_ref, x_ref, w_ref, *refs):
    pieces, (out_ref, lhs_ref, rows_ref, sum_ref) = refs[:-4], refs[-4:]
    me = me_ref[0]
    rows_ref[...] = x_ref[...].astype(jnp.float32)
    for p, b in enumerate(near_order):
        at = pl.ds(pl.multiple_of((me ^ b) * BLOCK, BLOCK), BLOCK)
        out_ref[at, :] = rows_ref[at, :] + near_ref[p * BLOCK : (p + 1) * BLOCK, :]
    unfold(lhs_ref, pieces)
    sum_ref[...] = jnp.dot(lhs_ref[...], w_ref[...], preferred_element_type=jnp.float32)
    for p, b in enumerate(far_order):
        at = pl.ds(pl.multiple_of((me ^ b) * BLOCK, BLOCK), BLOCK)
        out_ref[at, :] = rows_ref[at, :] + sum_ref[p * BLOCK : (p + 1) * BLOCK, :]


def far_output(me, orders, near, pieces, residual, w_output):
    total, width = residual.shape
    rows = len(pieces) * BLOCK
    return pl.pallas_call(
        functools.partial(far_output_kernel, *orders),
        in_specs=[SMEM] + [VMEM] * (3 + len(pieces)),
        out_specs=VMEM,
        out_shape=struct((total, width), jnp.float32),
        scratch_shapes=[
            pltpu.VMEM((rows, w_output.shape[0]), jnp.bfloat16),
            pltpu.VMEM((total, width), jnp.float32),
            pltpu.VMEM((rows, width), jnp.float32),
        ],
        compiler_params=pltpu.CompilerParams(vmem_limit_bytes=24 * 2**20),
        name="far_output",
    )(me, near, residual, w_output, *pieces)


def local(
    residual, norm_gain, w_query, w_keyval, w_output, key_cache, value_cache, lengths, positions
):
    count = lax.axis_size("gx")
    me = lax.axis_index("gx").astype(jnp.int32).reshape(1)
    heads = w_query.shape[1] // HD
    groups = count // (2 * QUAD)
    quad_masks = [2 * q for q in range(1, QUAD)]
    far_masks = [2 * QUAD * g for g in range(1, groups)]
    order = [
        core + 2 * q + 2 * QUAD * g for core in range(2) for g in range(groups) for q in range(QUAD)
    ]
    tables = rope_tables(positions)

    keep, send, stats, extra = project(me, order, residual, norm_gain, w_query, w_keyval)
    recv = exchange(send, 1, count)
    other = exchange(extra, 1, count)
    own, far, own_stats, far_stats, side, *sends = first_combine(keep, recv, stats, extra, other)
    w_output, token = load(w_output, own_stats)
    early = [exchange(v, m, count) for v, m in zip(sends[: QUAD - 1], quad_masks)]
    summed, *far_sends = far_combine(far, far_stats, side, early, token)
    late = [exchange(v, m, count) for v, m in zip(sends[QUAD - 1 :], quad_masks)]
    far_sums = [exchange(v, m, count) for v, m in zip(far_sends, far_masks)]
    attended, new_keyval = attend(
        lengths, own, own_stats, side, summed, tables, key_cache, value_cache, early, late,
        far_sums, heads,
    )

    far_pieces = [exchange(attended, m, count) for m in far_masks]
    near_pieces = [attended] + [exchange(attended, m, count) for m in quad_masks]
    far_pieces = [
        piece if mask == 0 else exchange(piece, mask, count)
        for piece in far_pieces
        for mask in [0] + quad_masks
    ]
    near_order = [core + 2 * q for core in range(2) for q in range(QUAD)]
    far_order = [
        core + 2 * q + 2 * QUAD * g
        for core in range(2)
        for g in range(1, groups)
        for q in range(QUAD)
    ]
    near_pieces += [exchange(p, 1, count) for p in near_pieces]
    far_pieces += [exchange(p, 1, count) for p in far_pieces]
    near = near_output(near_pieces, w_output)
    updated = far_output(me, (near_order, far_order), near, far_pieces, residual, w_output)
    return (updated, new_keyval)


def solution(mesh):
    in_specs = (
        P("groups", "gx"),
        P("gx"),
        P("gx", None),
        P("gx", None),
        P(None, "gx"),
        P(("groups", "gx"), None, None),
        P(("groups", "gx"), None, None),
        P(("groups", "gx")),
        P(("groups", "gx")),
    )
    out_specs = (P("groups", "gx"), P(("groups", "gx"), None))
    return jax.shard_map(local, mesh=mesh, in_specs=in_specs, out_specs=out_specs, check_vma=False)
```

```python
import functools
import math

import jax
import jax.numpy as jnp
from jax import lax
from jax.experimental import pallas as pl
from jax.experimental.pallas import tpu as pltpu
from jax.sharding import PartitionSpec as P

HD = 256
LANES = 128
BLOCK = 8
TILE = 512
SIDE = 32
AHEAD = 3
PACE = 1
QUAD = 4
PARTS = 4
EPSILON = 1e-05
VMEM = pl.BlockSpec(memory_space=pltpu.VMEM)
SMEM = pl.BlockSpec(memory_space=pltpu.SMEM)


def rope_tables(position_rows):
    half_width = HD // 2
    inverse_freq = 10000.0 ** (-(jnp.arange(half_width, dtype=jnp.float32) * 2.0 / HD))
    angles = position_rows.astype(jnp.float32)[:, None] * inverse_freq[None, :]
    return (jnp.cos(angles), jnp.sin(angles))


def exchange(value, mask, count):
    return lax.ppermute(value, "gx", [(i, i ^ mask) for i in range(count)])


def behind(value, first):
    return lax.optimization_barrier((value, first))[0]


def in_hbm(value):
    return pltpu.with_memory_space_constraint(value, pltpu.HBM)


def struct(shape, dtype):
    return jax.ShapeDtypeStruct(shape, dtype)


def lane_ids(rows):
    return lax.broadcasted_iota(jnp.int32, (rows, LANES), 1)


def pack_stats(stats):
    high = stats.astype(jnp.bfloat16).astype(jnp.float32)
    middle = (stats - high).astype(jnp.bfloat16).astype(jnp.float32)
    low = stats - high - middle
    lane = lane_ids(stats.shape[0])
    return jnp.where(lane < 2, high, jnp.where(lane < 4, middle, low)).astype(jnp.bfloat16)


def unpack_stats(packed):
    parts = packed.astype(jnp.float32)
    mean = parts[:, 0:1] + parts[:, 2:3] + parts[:, 4:5]
    square = parts[:, 1:2] + parts[:, 3:4] + parts[:, 5:6]
    return jnp.where(lane_ids(parts.shape[0]) % 2 == 0, mean, square)


def pack_side(side):
    pieces = []
    for start in range(0, SIDE, BLOCK):
        pieces.append(
            jnp.concatenate(
                [side[start : start + BLOCK], side[SIDE + start : SIDE + start + BLOCK]], axis=0
            )
        )
    return jnp.concatenate(pieces, axis=1)


def folded_row(packed, c):
    part = packed[:, c // BLOCK * LANES : (c // BLOCK + 1) * LANES]
    k = c % BLOCK
    upper = lax.broadcasted_iota(jnp.int32, (2 * BLOCK, LANES), 0) >= BLOCK
    return jnp.where(upper, part[BLOCK + k : BLOCK + k + 1], part[k : k + 1])


def merge_stats(parts):
    merged = sum(parts[1:], parts[0]) * (1.0 / len(parts))
    return merged, [p[:, 0:1] - merged[:, 0:1] for p in parts]


def project_kernel(order, me_ref, x_hbm, gain_hbm, wq_hbm, wkv_hbm, keep_ref, send_ref, stats_ref,
                   extra_ref, x_ref, gain_ref, rows_ref, lhs_ref, w_ref, in_sem, w_sem):
    total = x_ref.shape[0]
    half = total // 2
    me = me_ref[0]
    tiles = w_ref.shape[0]
    x_copy = pltpu.make_async_copy(x_hbm, x_ref, in_sem.at[0])
    gain_copy = pltpu.make_async_copy(gain_hbm, gain_ref, in_sem.at[1])
    x_copy.start()
    gain_copy.start()
    copies = []
    for t in range(tiles):
        source = wkv_hbm if t == 0 else wq_hbm.at[:, (t - 1) * TILE : t * TILE]
        copies.append(pltpu.make_async_copy(source, w_ref.at[t], w_sem.at[t]))
    started = min(AHEAD, tiles)
    for t in range(started):
        copies[t].start()
    x_copy.wait()
    gain_copy.wait()
    rows_ref[...] = x_ref[...].astype(jnp.float32)
    gain = gain_ref[...].reshape(1, gain_ref.shape[0])
    high = gain.astype(jnp.bfloat16).astype(jnp.float32)
    low = gain - high
    row = lax.broadcasted_iota(jnp.int32, (16, gain.shape[1]), 0)
    lhs_ref[total:, :] = jnp.where(
        row == 0, high, jnp.where(row == 1, low, 0.0)
    ).astype(jnp.bfloat16)
    lane = lane_ids(2 * BLOCK)
    extra_ref[half:, :] = jnp.zeros((2 * SIDE, LANES), jnp.float32)
    for pair in range(len(order) // 2):
        pieces = []
        for b in order[2 * pair : 2 * pair + 2]:
            start = pl.multiple_of((me ^ b) * BLOCK, BLOCK)
            pieces.append(rows_ref[pl.ds(start, BLOCK), :])
        x = jnp.concatenate(pieces, axis=0)
        mean = jnp.mean(x, axis=1, keepdims=True)
        square = jnp.mean(x * x, axis=1, keepdims=True)
        at = pair * 2 * BLOCK
        lhs_ref[at : at + 2 * BLOCK, :] = ((x - mean) * gain).astype(jnp.bfloat16)
        if started < tiles - 1 and pair % PACE == PACE - 1:
            copies[started].start()
            started += 1
        stats = jnp.where(lane % 2 == 0, mean, square)
        if at < half:
            stats_ref[at : at + 2 * BLOCK, :] = stats
        else:
            extra_ref[at - half : at - half + 2 * BLOCK, :] = stats

    chunks = tiles * (TILE // LANES) // 2
    for t in range(tiles):
        while started < min(tiles, t + AHEAD + 4):
            copies[started].start()
            started += 1
        copies[t].wait()
        out = jnp.dot(lhs_ref[...], w_ref[t], preferred_element_type=jnp.float32)
        columns = slice(t * TILE, (t + 1) * TILE)
        keep_ref[:, columns] = out[:half]
        send_ref[:, columns] = out[half:total].astype(jnp.bfloat16)
        gained = out[total : total + 1] + out[total + 1 : total + 2]
        for k in range(TILE // LANES):
            c = t * (TILE // LANES) + k
            at = half + c if c < chunks else half + SIDE + c - chunks
            extra_ref[at : at + 1, :] = gained[:, k * LANES : (k + 1) * LANES]


def project(me, order, residual, gain, w_query, w_keyval):
    total, depth = residual.shape
    width = w_query.shape[1] + w_keyval.shape[1]
    half = total // 2
    tiles = width // TILE
    return pl.pallas_call(
        functools.partial(project_kernel, order),
        in_specs=[SMEM] + [pl.BlockSpec(memory_space=pltpu.HBM)] * 4,
        out_specs=[VMEM] * 4,
        out_shape=[
            struct((half, width), jnp.float32),
            struct((half, width), jnp.bfloat16),
            struct((half, LANES), jnp.float32),
            struct((half + 2 * SIDE, LANES), jnp.float32),
        ],
        scratch_shapes=[
            pltpu.VMEM((total, depth), jnp.bfloat16),
            pltpu.VMEM((depth,), jnp.float32),
            pltpu.VMEM((total, depth), jnp.float32),
            pltpu.VMEM((total + 16, depth), jnp.bfloat16),
            pltpu.VMEM((tiles, depth, TILE), jnp.bfloat16),
            pltpu.SemaphoreType.DMA((2,)),
            pltpu.SemaphoreType.DMA((tiles,)),
        ],
        compiler_params=pltpu.CompilerParams(vmem_limit_bytes=24 * 2**20),
        name="project",
    )(me, *(in_hbm(v) for v in (residual, gain, w_query, w_keyval)))


def first_kernel(keep_ref, recv_ref, stats_ref, extra_ref, other_ref,
                 own_ref, far_ref, own_stats, far_stats, side_ref, *send_refs):
    half, width = keep_ref.shape
    cut = width // 2
    chunks = cut // LANES
    early, late = send_refs[: QUAD - 1], send_refs[QUAD - 1 :]
    own = stats_ref[...]
    other = other_ref[:half, :]
    merged = 0.5 * (own + other)
    shift = 0.5 * (own[:, 0:1] - other[:, 0:1])
    side = extra_ref[half:, :] + other_ref[half:, :]
    change = extra_ref[half:, :] - other_ref[half:, :]
    side_ref[...] = side
    packed_side = pack_side(side).astype(jnp.bfloat16)
    fold = 2 * BLOCK

    def target(k):
        group, q = divmod(k, QUAD)
        return group, q, slice((group - 1) * fold, group * fold)

    for k in range(half // BLOCK):
        group, q, at = target(k)
        stats = merged[k * BLOCK : (k + 1) * BLOCK]
        stats = jnp.concatenate([stats, stats], axis=0)
        if q == 0:
            if group == 0:
                own_stats[...] = stats
            else:
                far_stats[at, :] = stats
        elif group == 0:
            late[q - 1][:, cut:] = pack_stats(stats)
        else:
            early[q - 1][at, cut : cut + LANES] = pack_stats(stats)
            early[q - 1][at, cut + LANES :] = packed_side
    for c in range(chunks):
        columns = slice(c * LANES, (c + 1) * LANES)
        totals = []
        for n in range(2):
            source = slice(n * cut + c * LANES, n * cut + (c + 1) * LANES)
            row = n * SIDE + c
            totals.append(
                keep_ref[:, source]
                + recv_ref[:, source].astype(jnp.float32)
                + shift * change[row : row + 1]
            )
        for k in range(half // BLOCK):
            group, q, at = target(k)
            value = jnp.concatenate([t[k * BLOCK : (k + 1) * BLOCK] for t in totals], axis=0)
            if q == 0:
                if group == 0:
                    own_ref[:, columns] = value
                else:
                    far_ref[at, columns] = value
            elif group == 0:
                late[q - 1][:, columns] = value.astype(jnp.bfloat16)
            else:
                early[q - 1][at, columns] = value.astype(jnp.bfloat16)


def first_combine(keep, recv, stats, extra, other):
    half, width = keep.shape
    cut = width // 2
    fold = 2 * BLOCK
    groups = half // (QUAD * BLOCK)
    far = (groups - 1) * fold
    return pl.pallas_call(
        first_kernel,
        in_specs=[VMEM] * 5,
        out_specs=[VMEM] * (5 + 2 * (QUAD - 1)),
        out_shape=[
            struct((fold, cut), jnp.float32),
            struct((far, cut), jnp.float32),
            struct((fold, LANES), jnp.float32),
            struct((far, LANES), jnp.float32),
            struct((2 * SIDE, LANES), jnp.float32),
        ]
        + [struct((far, cut + LANES + SIDE // BLOCK * LANES), jnp.bfloat16)] * (QUAD - 1)
        + [struct((fold, cut + LANES), jnp.bfloat16)] * (QUAD - 1),
        compiler_params=pltpu.CompilerParams(vmem_limit_bytes=16 * 2**20),
        name="first_combine",
    )(keep, recv, stats, extra, other)


def far_add_kernel(far_ref, recv_ref, out_ref):
    cut = far_ref.shape[1]
    out_ref[...] = far_ref[...] + recv_ref[:, :cut].astype(jnp.float32)


def far_add(far, recv):
    return pl.pallas_call(
        far_add_kernel,
        in_specs=[VMEM] * 2,
        out_specs=VMEM,
        out_shape=struct(far.shape, far.dtype),
        compiler_params=pltpu.CompilerParams(vmem_limit_bytes=16 * 2**20),
        name="far_add",
    )(far, recv)


def far_kernel(far_ref, stats_ref, side_ref, *refs):
    recv, outs = refs[: QUAD - 1], refs[QUAD - 1 :]
    cut = far_ref.shape[1]
    fold = 2 * BLOCK
    packed = [r[:fold, cut + LANES :].astype(jnp.float32) for r in recv]
    packed = [pack_side(side_ref[...])] + packed
    summed = sum(packed[1:], packed[0])
    outs[0][...] = summed
    for g, out in enumerate(outs[1:]):
        at = slice(g * fold, (g + 1) * fold)
        parts = [stats_ref[at, :]] + [unpack_stats(r[at, cut : cut + LANES]) for r in recv]
        merged, shifts = merge_stats(parts)
        out[:, cut : cut + LANES] = pack_stats(merged)
        out[:, cut + LANES :] = summed.astype(jnp.bfloat16)
        for c in range(cut // LANES):
            columns = slice(c * LANES, (c + 1) * LANES)
            total = far_ref[at, columns]
            for r in recv[:-1]:
                total = total + r[at, columns].astype(jnp.float32)
            for shift, side in zip(shifts, packed):
                total = total + shift * folded_row(side, c)
            out[:, columns] = total.astype(jnp.bfloat16)


def far_combine(far, stats, side, recv):
    cut = far.shape[1]
    fold = 2 * BLOCK
    groups = far.shape[0] // fold
    side_columns = SIDE // BLOCK * LANES
    return pl.pallas_call(
        far_kernel,
        in_specs=[VMEM] * (3 + QUAD - 1),
        out_specs=[VMEM] * (1 + groups),
        out_shape=[struct((fold, side_columns), jnp.float32)]
        + [struct((fold, cut + LANES + side_columns), jnp.bfloat16)] * groups,
        compiler_params=pltpu.CompilerParams(vmem_limit_bytes=16 * 2**20),
        name="far_combine",
    )(far, stats, side, *recv)


def two_part_dot(left, right, dims):
    rows = left.shape[0]
    high = left.astype(jnp.bfloat16)
    low = (left - high.astype(jnp.float32)).astype(jnp.bfloat16)
    both = jnp.concatenate([high.astype(jnp.float32), low.astype(jnp.float32)], axis=0)
    out = lax.dot_general(
        both.astype(jnp.bfloat16), right, dims, preferred_element_type=jnp.float32
    )
    return out[:rows] + out[rows:]


def attend_kernel(heads, length_ref, after_ref, own_ref, stats_ref, side_ref, summed_ref, cos_ref, sin_ref,
                  key_ref, value_ref, *refs):
    early, late = refs[: QUAD - 1], refs[QUAD - 1 : 2 * QUAD - 2]
    far, (attended_ref, keyval_ref, q_ref, out_ref) = refs[2 * QUAD - 2 : -4], refs[-4:]
    cut = own_ref.shape[1]
    chunks = cut // LANES
    slots = key_ref.shape[1]
    fold = 2 * BLOCK
    parts = [stats_ref[...]] + [unpack_stats(r[:, cut:]) for r in late]
    merged, near_shifts = merge_stats(parts)
    packed = [pack_side(side_ref[...])]
    packed += [r[:fold, cut + LANES :].astype(jnp.float32) for r in early]
    parts = [merged] + [unpack_stats(r[:, cut : cut + LANES]) for r in far]
    merged, far_shifts = merge_stats(parts)
    packed += [summed_ref[...]] + [r[:, cut + LANES :].astype(jnp.float32) for r in far]
    shifts = near_shifts + far_shifts
    mean, square = merged[:, 0:1], merged[:, 1:2]
    scale = lax.rsqrt(square - mean * mean + EPSILON)
    cosine, sine = cos_ref[...], sin_ref[...]
    new_key = new_value = None
    for c in range(0, chunks, 2):
        pair = []
        for d in (c, c + 1):
            columns = slice(d * LANES, (d + 1) * LANES)
            total = own_ref[:, columns]
            for r in (*late, *far):
                total = total + r[:, columns].astype(jnp.float32)
            for shift, side in zip(shifts, packed):
                total = total + shift * folded_row(side, d)
            pair.append(total * scale)
        for half in range(2):
            u1, u2 = (v[half * BLOCK : (half + 1) * BLOCK] for v in pair)
            number = half * (chunks // 2) + c // 2 - 2
            if number == -1:
                new_value = jnp.concatenate([u1, u2], axis=1)
                continue
            turned = (u1 * cosine - u2 * sine, u2 * cosine + u1 * sine)
            if number == -2:
                new_key = jnp.concatenate(turned, axis=1)
            else:
                for k in range(2):
                    q_ref[k, number * BLOCK : (number + 1) * BLOCK, :] = turned[k]
    keyval_ref[:, :HD] = new_key
    keyval_ref[:, HD:] = new_value
    factor = 1.0 / math.sqrt(HD)
    slot = lax.broadcasted_iota(jnp.int32, (heads, slots), 1)
    key_rounded = new_key.astype(jnp.bfloat16).astype(jnp.float32)
    value_rounded = new_value.astype(jnp.bfloat16).astype(jnp.float32)
    requests = range(BLOCK)
    queries = [
        jnp.concatenate(
            [q_ref.at[k][pl.ds(r, heads, stride=BLOCK), :] for k in range(2)], axis=1
        )
        for r in requests
    ]
    scores = [
        two_part_dot(queries[r], key_ref[r], (((1,), (1,)), ((), ()))) for r in requests
    ]
    own_scores = [
        jnp.sum(queries[r] * key_rounded[r : r + 1], axis=1, keepdims=True)
        * factor
        for r in requests
    ]
    masked = [jnp.where(slot < length_ref[r], scores[r] * factor, -jnp.inf) for r in requests]
    highest = [
        jnp.maximum(jnp.max(masked[r], axis=1, keepdims=True), own_scores[r]) for r in requests
    ]
    exps = [jnp.exp(masked[r] - highest[r]) for r in requests]
    own_exps = [jnp.exp(own_scores[r] - highest[r]) for r in requests]
    inverse = [
        1.0 / (jnp.sum(exps[r], axis=1, keepdims=True) + own_exps[r]) for r in requests
    ]
    mixed = [
        two_part_dot(exps[r], value_ref[r], (((1,), (0,)), ((), ()))) * inverse[r] for r in requests
    ]
    for r in requests:
        own_weight = own_exps[r] * inverse[r]
        result = mixed[r] + own_weight * value_rounded[r : r + 1]
        for k in range(2):
            out_ref.at[k][pl.ds(r, heads, stride=BLOCK), :] = result[:, k * LANES : (k + 1) * LANES]
    for h in range(heads // 2):
        upper_head = h + heads // 2
        for k in range(2):
            at = h * HD + k * LANES
            attended_ref[:, at : at + LANES] = jnp.concatenate(
                [out_ref[k, g * BLOCK : (g + 1) * BLOCK, :] for g in (h, upper_head)], axis=0
            ).astype(jnp.bfloat16)


def attend(lengths, after, own, stats, side, summed, tables, key_cache, value_cache, early, late, far,
           heads):
    return pl.pallas_call(
        functools.partial(attend_kernel, heads),
        in_specs=[SMEM, pl.BlockSpec(memory_space=pl.ANY)]
        + [VMEM] * (8 + len(early) + len(late) + len(far)),
        out_specs=[VMEM] * 2,
        out_shape=[
            struct((2 * BLOCK, heads * HD // 2), jnp.bfloat16),
            struct((BLOCK, 2 * HD), jnp.float32),
        ],
        scratch_shapes=[
            pltpu.VMEM((2, heads * BLOCK, LANES), jnp.float32),
            pltpu.VMEM((2, heads * BLOCK, LANES), jnp.float32),
        ],
        compiler_params=pltpu.CompilerParams(vmem_limit_bytes=24 * 2**20),
        name="attend",
    )(
        lengths, after, own, stats, side, summed, *tables, key_cache, value_cache, *early, *late, *far
    )


def load_kernel(w_hbm, after_ref, out_ref, token_ref, sems):
    parts = sems.shape[0]
    rows = out_ref.shape[0] // parts
    copies = [
        pltpu.make_async_copy(
            w_hbm.at[k * rows : (k + 1) * rows, :], out_ref.at[k * rows : (k + 1) * rows, :], sems.at[k]
        )
        for k in range(parts)
    ]
    for copy in copies:
        copy.start()
    for copy in copies:
        copy.wait()
    token_ref[...] = jnp.zeros_like(token_ref)


def load(w_output, after):
    return pl.pallas_call(
        load_kernel,
        in_specs=[pl.BlockSpec(memory_space=pltpu.HBM), pl.BlockSpec(memory_space=pl.ANY)],
        out_specs=[VMEM] * 2,
        out_shape=[
            struct((w_output.shape[0] // 2, w_output.shape[1]), w_output.dtype),
            struct((BLOCK, LANES), jnp.float32),
        ],
        scratch_shapes=[pltpu.SemaphoreType.DMA((PARTS,))],
        compiler_params=pltpu.CompilerParams(vmem_limit_bytes=16 * 2**20),
        cost_estimate=pl.CostEstimate(
            flops=0, bytes_accessed=w_output.size, transcendentals=0
        ),
        name="load",
    )(in_hbm(w_output), after)


def unfold(lhs_ref, pieces):
    cut = pieces[0].shape[1]
    for k in range(0, len(pieces), 2):
        pair = [p[...].astype(jnp.float32) for p in pieces[k : k + 2]]
        at = slice(k * BLOCK, (k + 2) * BLOCK)
        lhs_ref[at, :cut] = jnp.concatenate([p[:BLOCK] for p in pair], axis=0).astype(jnp.bfloat16)
        lhs_ref[at, cut:] = jnp.concatenate([p[BLOCK:] for p in pair], axis=0).astype(jnp.bfloat16)


def near_output_kernel(first_ref, w_hbm, *refs):
    pieces, (out_ref, second_ref, lhs_ref, sems) = refs[:-4], refs[-4:]
    depth = second_ref.shape[0]
    rows = depth // PARTS
    copies = [
        pltpu.make_async_copy(
            w_hbm.at[depth + k * rows : depth + (k + 1) * rows, :],
            second_ref.at[k * rows : (k + 1) * rows, :],
            sems.at[k],
        )
        for k in range(PARTS)
    ]
    for copy in copies:
        copy.start()
    unfold(lhs_ref, pieces)
    out_ref[...] = jnp.dot(
        lhs_ref[:, :depth], first_ref[...], preferred_element_type=jnp.float32
    )
    for k in range(PARTS):
        copies[k].wait()
        out_ref[...] += jnp.dot(
            lhs_ref[:, depth + k * rows : depth + (k + 1) * rows],
            second_ref[k * rows : (k + 1) * rows, :],
            preferred_element_type=jnp.float32,
        )


def near_output(pieces, first, w_output):
    rows = len(pieces) * BLOCK
    depth, width = w_output.shape
    return pl.pallas_call(
        near_output_kernel,
        in_specs=[VMEM, pl.BlockSpec(memory_space=pltpu.HBM)] + [VMEM] * len(pieces),
        out_specs=[VMEM] * 2,
        out_shape=[
            struct((rows, width), jnp.float32),
            struct((depth // 2, width), w_output.dtype),
        ],
        scratch_shapes=[
            pltpu.VMEM((rows, depth), jnp.bfloat16),
            pltpu.SemaphoreType.DMA((PARTS,)),
        ],
        compiler_params=pltpu.CompilerParams(vmem_limit_bytes=24 * 2**20),
        cost_estimate=pl.CostEstimate(
            flops=2 * rows * depth * width, bytes_accessed=w_output.size, transcendentals=0
        ),
        name="near_output",
    )(first, in_hbm(w_output), *pieces)


def far_output_kernel(near_order, far_order, me_ref, near_ref, x_ref, first_ref, second_ref, *refs):
    pieces, (out_ref, lhs_ref, rows_ref, sum_ref) = refs[:-4], refs[-4:]
    me = me_ref[0]
    rows_ref[...] = x_ref[...].astype(jnp.float32)
    for p, b in enumerate(near_order):
        at = pl.ds(pl.multiple_of((me ^ b) * BLOCK, BLOCK), BLOCK)
        out_ref[at, :] = rows_ref[at, :] + near_ref[p * BLOCK : (p + 1) * BLOCK, :]
    unfold(lhs_ref, pieces)
    depth = first_ref.shape[0]
    sum_ref[...] = jnp.dot(
        lhs_ref[:, :depth], first_ref[...], preferred_element_type=jnp.float32
    ) + jnp.dot(lhs_ref[:, depth:], second_ref[...], preferred_element_type=jnp.float32)
    for p, b in enumerate(far_order):
        at = pl.ds(pl.multiple_of((me ^ b) * BLOCK, BLOCK), BLOCK)
        out_ref[at, :] = rows_ref[at, :] + sum_ref[p * BLOCK : (p + 1) * BLOCK, :]


def far_output(me, orders, near, pieces, residual, weights):
    total, width = residual.shape
    rows = len(pieces) * BLOCK
    return pl.pallas_call(
        functools.partial(far_output_kernel, *orders),
        in_specs=[SMEM] + [VMEM] * (4 + len(pieces)),
        out_specs=VMEM,
        out_shape=struct((total, width), jnp.float32),
        scratch_shapes=[
            pltpu.VMEM((rows, 2 * weights[0].shape[0]), jnp.bfloat16),
            pltpu.VMEM((total, width), jnp.float32),
            pltpu.VMEM((rows, width), jnp.float32),
        ],
        compiler_params=pltpu.CompilerParams(vmem_limit_bytes=24 * 2**20),
        name="far_output",
    )(me, near, residual, *weights, *pieces)


def local(
    residual, norm_gain, w_query, w_keyval, w_output, key_cache, value_cache, lengths, positions
):
    count = lax.axis_size("gx")
    me = lax.axis_index("gx").astype(jnp.int32).reshape(1)
    heads = w_query.shape[1] // HD
    groups = count // (2 * QUAD)
    quad_masks = [2 * q for q in range(1, QUAD)]
    far_masks = [2 * QUAD * g for g in range(1, groups)]
    order = [
        core + 2 * q + 2 * QUAD * g for core in range(2) for g in range(groups) for q in range(QUAD)
    ]
    tables = rope_tables(positions)

    keep, send, stats, extra = project(me, order, residual, norm_gain, w_query, w_keyval)
    recv = exchange(send, 1, count)
    other = exchange(extra, 1, count)
    own, far, own_stats, far_stats, side, *sends = first_combine(keep, recv, stats, extra, other)
    early = [exchange(v, m, count) for v, m in zip(sends[: QUAD - 1], quad_masks)]
    far = far_add(far, early[-1])
    summed, *far_sends = far_combine(far, far_stats, side, early)
    late = [exchange(v, m, count) for v, m in zip(sends[QUAD - 1 :], quad_masks)]
    first, token = load(w_output, summed)
    far_sums = [exchange(v, m, count) for v, m in zip(far_sends, far_masks)]
    attended, new_keyval = attend(
        lengths, token, own, own_stats, side, summed, tables, key_cache, value_cache, early, late,
        far_sums, heads,
    )

    far_pieces = [exchange(attended, m, count) for m in far_masks]
    copied = attended
    near_pieces = [attended] + [exchange(copied, m, count) for m in quad_masks]
    far_pieces = [
        piece if mask == 0 else exchange(piece, mask, count)
        for piece in far_pieces
        for mask in [0] + quad_masks
    ]
    near_order = [core + 2 * q for core in range(2) for q in range(QUAD)]
    far_order = [
        core + 2 * q + 2 * QUAD * g
        for core in range(2)
        for g in range(1, groups)
        for q in range(QUAD)
    ]
    near_pieces += [exchange(behind(p, far_pieces[0]), 1, count) for p in near_pieces]
    near, second = near_output(near_pieces, first, w_output)
    far_pieces += [
        exchange(p if k % QUAD == 0 else behind(p, near), 1, count)
        for k, p in enumerate(far_pieces)
    ]
    updated = far_output(
        me, (near_order, far_order), near, far_pieces, residual, (first, second)
    )
    return (updated, new_keyval)


def solution(mesh):
    in_specs = (
        P("groups", "gx"),
        P("gx"),
        P("gx", None),
        P("gx", None),
        P(None, "gx"),
        P(("groups", "gx"), None, None),
        P(("groups", "gx"), None, None),
        P(("groups", "gx")),
        P(("groups", "gx")),
    )
    out_specs = (P("groups", "gx"), P(("groups", "gx"), None))
    return jax.shard_map(local, mesh=mesh, in_specs=in_specs, out_specs=out_specs, check_vma=False)
```

```python
import functools
import math

import jax
import jax.numpy as jnp
from jax import lax
from jax.experimental import pallas as pl
from jax.experimental.pallas import tpu as pltpu
from jax.sharding import PartitionSpec as P

HD = 256
LANES = 128
BLOCK = 8
TILE = 512
WIDE = 1024
SIDE = 32
AHEAD = 3
PACE = 1
QUAD = 4
PARTS = 4
LOADS = (11, 16)
EPSILON = 1e-05
VMEM = pl.BlockSpec(memory_space=pltpu.VMEM)
SMEM = pl.BlockSpec(memory_space=pltpu.SMEM)


def rope_tables(position_rows):
    half_width = HD // 2
    inverse_freq = 10000.0 ** (-(jnp.arange(half_width, dtype=jnp.float32) * 2.0 / HD))
    angles = position_rows.astype(jnp.float32)[:, None] * inverse_freq[None, :]
    return (jnp.cos(angles), jnp.sin(angles))


def exchange(value, mask, count):
    return lax.ppermute(value, "gx", [(i, i ^ mask) for i in range(count)])


def behind(value, first):
    return lax.optimization_barrier((value, first))[0]


def in_hbm(value):
    return pltpu.with_memory_space_constraint(value, pltpu.HBM)


def struct(shape, dtype):
    return jax.ShapeDtypeStruct(shape, dtype)


def lane_ids(rows):
    return lax.broadcasted_iota(jnp.int32, (rows, LANES), 1)


def pack_stats(stats):
    high = stats.astype(jnp.bfloat16).astype(jnp.float32)
    middle = (stats - high).astype(jnp.bfloat16).astype(jnp.float32)
    low = stats - high - middle
    lane = lane_ids(stats.shape[0])
    return jnp.where(lane < 2, high, jnp.where(lane < 4, middle, low)).astype(jnp.bfloat16)


def unpack_stats(packed):
    parts = packed.astype(jnp.float32)
    mean = parts[:, 0:1] + parts[:, 2:3] + parts[:, 4:5]
    square = parts[:, 1:2] + parts[:, 3:4] + parts[:, 5:6]
    return jnp.where(lane_ids(parts.shape[0]) % 2 == 0, mean, square)


def pack_side(side):
    pieces = []
    for start in range(0, SIDE, BLOCK):
        pieces.append(
            jnp.concatenate(
                [side[start : start + BLOCK], side[SIDE + start : SIDE + start + BLOCK]], axis=0
            )
        )
    return jnp.concatenate(pieces, axis=1)


def folded_row(packed, c):
    part = packed[:, c // BLOCK * LANES : (c // BLOCK + 1) * LANES]
    k = c % BLOCK
    upper = lax.broadcasted_iota(jnp.int32, (2 * BLOCK, LANES), 0) >= BLOCK
    return jnp.where(upper, part[BLOCK + k : BLOCK + k + 1], part[k : k + 1])


def merge_stats(parts):
    merged = sum(parts[1:], parts[0]) * (1.0 / len(parts))
    return merged, [p[:, 0:1] - merged[:, 0:1] for p in parts]


def project_kernel(order, me_ref, x_hbm, gain_hbm, wq_hbm, wkv_hbm, keep_ref, send_ref, stats_ref,
                   extra_ref, x_ref, gain_ref, rows_ref, lhs_ref, wkv_ref, w_ref, in_sem,
                   w_sem):
    total = x_ref.shape[0]
    half = total // 2
    me = me_ref[0]
    tiles = w_sem.shape[0]
    x_copy = pltpu.make_async_copy(x_hbm, x_ref, in_sem.at[0])
    gain_copy = pltpu.make_async_copy(gain_hbm, gain_ref, in_sem.at[1])
    x_copy.start()
    gain_copy.start()
    copies = []
    for t in range(tiles):
        if t == 0:
            source, target = wkv_hbm, wkv_ref
        else:
            source, target = wq_hbm.at[:, (t - 1) * WIDE : t * WIDE], w_ref.at[t - 1]
        copies.append(pltpu.make_async_copy(source, target, w_sem.at[t]))
    started = min(AHEAD, tiles)
    for t in range(started):
        copies[t].start()
    x_copy.wait()
    gain_copy.wait()
    rows_ref[...] = x_ref[...].astype(jnp.float32)
    gain = gain_ref[...].reshape(1, gain_ref.shape[0])
    high = gain.astype(jnp.bfloat16).astype(jnp.float32)
    low = gain - high
    row = lax.broadcasted_iota(jnp.int32, (16, gain.shape[1]), 0)
    lhs_ref[total:, :] = jnp.where(
        row == 0, high, jnp.where(row == 1, low, 0.0)
    ).astype(jnp.bfloat16)
    lane = lane_ids(2 * BLOCK)
    extra_ref[half:, :] = jnp.zeros((2 * SIDE, LANES), jnp.float32)
    for pair in range(len(order) // 2):
        pieces = []
        for b in order[2 * pair : 2 * pair + 2]:
            start = pl.multiple_of((me ^ b) * BLOCK, BLOCK)
            pieces.append(rows_ref[pl.ds(start, BLOCK), :])
        x = jnp.concatenate(pieces, axis=0)
        mean = jnp.mean(x, axis=1, keepdims=True)
        square = jnp.mean(x * x, axis=1, keepdims=True)
        at = pair * 2 * BLOCK
        lhs_ref[at : at + 2 * BLOCK, :] = ((x - mean) * gain).astype(jnp.bfloat16)
        if started < tiles - 1 and pair % PACE == PACE - 1:
            copies[started].start()
            started += 1
        stats = jnp.where(lane % 2 == 0, mean, square)
        if at < half:
            stats_ref[at : at + 2 * BLOCK, :] = stats
        else:
            extra_ref[at - half : at - half + 2 * BLOCK, :] = stats

    chunks = keep_ref.shape[1] // LANES // 2
    at_column = 0
    for t in range(tiles):
        while started < min(tiles, t + AHEAD + 4):
            copies[started].start()
            started += 1
        copies[t].wait()
        weights = wkv_ref if t == 0 else w_ref.at[t - 1]
        for start in range(0, weights.shape[1], TILE):
            out = jnp.dot(
                lhs_ref[...], weights[:, start : start + TILE], preferred_element_type=jnp.float32
            )
            columns = slice(at_column, at_column + TILE)
            keep_ref[:, columns] = out[:half]
            send_ref[:, columns] = out[half:total].astype(jnp.bfloat16)
            gained = out[total : total + 1] + out[total + 1 : total + 2]
            for k in range(TILE // LANES):
                c = at_column // LANES + k
                at = half + c if c < chunks else half + SIDE + c - chunks
                extra_ref[at : at + 1, :] = gained[:, k * LANES : (k + 1) * LANES]
            at_column += TILE


def project(me, order, residual, gain, w_query, w_keyval):
    total, depth = residual.shape
    width = w_query.shape[1] + w_keyval.shape[1]
    half = total // 2
    return pl.pallas_call(
        functools.partial(project_kernel, order),
        in_specs=[SMEM] + [pl.BlockSpec(memory_space=pltpu.HBM)] * 4,
        out_specs=[VMEM] * 4,
        out_shape=[
            struct((half, width), jnp.float32),
            struct((half, width), jnp.bfloat16),
            struct((half, LANES), jnp.float32),
            struct((half + 2 * SIDE, LANES), jnp.float32),
        ],
        scratch_shapes=[
            pltpu.VMEM((total, depth), jnp.bfloat16),
            pltpu.VMEM((depth,), jnp.float32),
            pltpu.VMEM((total, depth), jnp.float32),
            pltpu.VMEM((total + 16, depth), jnp.bfloat16),
            pltpu.VMEM((depth, w_keyval.shape[1]), jnp.bfloat16),
            pltpu.VMEM((w_query.shape[1] // WIDE, depth, WIDE), jnp.bfloat16),
            pltpu.SemaphoreType.DMA((2,)),
            pltpu.SemaphoreType.DMA((1 + w_query.shape[1] // WIDE,)),
        ],
        compiler_params=pltpu.CompilerParams(vmem_limit_bytes=24 * 2**20),
        name="project",
    )(me, *(in_hbm(v) for v in (residual, gain, w_query, w_keyval)))


def first_kernel(keep_ref, recv_ref, stats_ref, extra_ref, other_ref,
                 own_ref, far_ref, own_stats, far_stats, side_ref, *send_refs):
    half, width = keep_ref.shape
    cut = width // 2
    chunks = cut // LANES
    early, late = send_refs[: QUAD - 1], send_refs[QUAD - 1 :]
    own = stats_ref[...]
    other = other_ref[:half, :]
    merged = 0.5 * (own + other)
    shift = 0.5 * (own[:, 0:1] - other[:, 0:1])
    side = extra_ref[half:, :] + other_ref[half:, :]
    change = extra_ref[half:, :] - other_ref[half:, :]
    side_ref[...] = side
    packed_side = pack_side(side).astype(jnp.bfloat16)
    fold = 2 * BLOCK

    def target(k):
        group, q = divmod(k, QUAD)
        return group, q, slice((group - 1) * fold, group * fold)

    for k in range(half // BLOCK):
        group, q, at = target(k)
        stats = merged[k * BLOCK : (k + 1) * BLOCK]
        stats = jnp.concatenate([stats, stats], axis=0)
        if q == 0:
            if group == 0:
                own_stats[...] = stats
            else:
                far_stats[at, :] = stats
        elif group == 0:
            late[q - 1][:, cut:] = pack_stats(stats)
        else:
            early[q - 1][at, cut : cut + LANES] = pack_stats(stats)
            early[q - 1][at, cut + LANES :] = packed_side
    for c in range(chunks):
        columns = slice(c * LANES, (c + 1) * LANES)
        totals = []
        for n in range(2):
            source = slice(n * cut + c * LANES, n * cut + (c + 1) * LANES)
            row = n * SIDE + c
            totals.append(
                keep_ref[:, source]
                + recv_ref[:, source].astype(jnp.float32)
                + shift * change[row : row + 1]
            )
        for k in range(half // BLOCK):
            group, q, at = target(k)
            value = jnp.concatenate([t[k * BLOCK : (k + 1) * BLOCK] for t in totals], axis=0)
            if q == 0:
                if group == 0:
                    own_ref[:, columns] = value
                else:
                    far_ref[at, columns] = value
            elif group == 0:
                late[q - 1][:, columns] = value.astype(jnp.bfloat16)
            else:
                early[q - 1][at, columns] = value.astype(jnp.bfloat16)


def first_combine(keep, recv, stats, extra, other):
    half, width = keep.shape
    cut = width // 2
    fold = 2 * BLOCK
    groups = half // (QUAD * BLOCK)
    far = (groups - 1) * fold
    return pl.pallas_call(
        first_kernel,
        in_specs=[VMEM] * 5,
        out_specs=[VMEM] * (5 + 2 * (QUAD - 1)),
        out_shape=[
            struct((fold, cut), jnp.float32),
            struct((far, cut), jnp.float32),
            struct((fold, LANES), jnp.float32),
            struct((far, LANES), jnp.float32),
            struct((2 * SIDE, LANES), jnp.float32),
        ]
        + [struct((far, cut + LANES + SIDE // BLOCK * LANES), jnp.bfloat16)] * (QUAD - 1)
        + [struct((fold, cut + LANES), jnp.bfloat16)] * (QUAD - 1),
        compiler_params=pltpu.CompilerParams(vmem_limit_bytes=16 * 2**20),
        name="first_combine",
    )(keep, recv, stats, extra, other)


def far_add_kernel(far_ref, recv_ref, out_ref):
    cut = far_ref.shape[1]
    out_ref[...] = far_ref[...] + recv_ref[:, :cut].astype(jnp.float32)


def far_add(far, recv):
    return pl.pallas_call(
        far_add_kernel,
        in_specs=[VMEM] * 2,
        out_specs=VMEM,
        out_shape=struct(far.shape, far.dtype),
        compiler_params=pltpu.CompilerParams(vmem_limit_bytes=16 * 2**20),
        name="far_add",
    )(far, recv)


def far_kernel(far_ref, stats_ref, side_ref, *refs):
    recv, outs = refs[: QUAD - 1], refs[QUAD - 1 :]
    cut = far_ref.shape[1]
    fold = 2 * BLOCK
    packed = [r[:fold, cut + LANES :].astype(jnp.float32) for r in recv]
    packed = [pack_side(side_ref[...])] + packed
    summed = sum(packed[1:], packed[0])
    outs[0][...] = summed
    for g, out in enumerate(outs[1:]):
        at = slice(g * fold, (g + 1) * fold)
        parts = [stats_ref[at, :]] + [unpack_stats(r[at, cut : cut + LANES]) for r in recv]
        merged, shifts = merge_stats(parts)
        out[:, cut : cut + LANES] = pack_stats(merged)
        out[:, cut + LANES :] = summed.astype(jnp.bfloat16)
        for c in range(cut // LANES):
            columns = slice(c * LANES, (c + 1) * LANES)
            total = far_ref[at, columns]
            for r in recv[:-1]:
                total = total + r[at, columns].astype(jnp.float32)
            for shift, side in zip(shifts, packed):
                total = total + shift * folded_row(side, c)
            out[:, columns] = total.astype(jnp.bfloat16)


def far_combine(far, stats, side, recv):
    cut = far.shape[1]
    fold = 2 * BLOCK
    groups = far.shape[0] // fold
    side_columns = SIDE // BLOCK * LANES
    return pl.pallas_call(
        far_kernel,
        in_specs=[VMEM] * (3 + QUAD - 1),
        out_specs=[VMEM] * (1 + groups),
        out_shape=[struct((fold, side_columns), jnp.float32)]
        + [struct((fold, cut + LANES + side_columns), jnp.bfloat16)] * groups,
        compiler_params=pltpu.CompilerParams(vmem_limit_bytes=16 * 2**20),
        name="far_combine",
    )(far, stats, side, *recv)


def two_part_dot(left, right, dims):
    rows = left.shape[0]
    high = left.astype(jnp.bfloat16)
    low = (left - high.astype(jnp.float32)).astype(jnp.bfloat16)
    both = jnp.concatenate([high.astype(jnp.float32), low.astype(jnp.float32)], axis=0)
    out = lax.dot_general(
        both.astype(jnp.bfloat16), right, dims, preferred_element_type=jnp.float32
    )
    return out[:rows] + out[rows:]


def attend_kernel(heads, length_ref, after_ref, own_ref, stats_ref, side_ref, summed_ref, cos_ref, sin_ref,
                  key_ref, value_ref, *refs):
    early, late = refs[: QUAD - 1], refs[QUAD - 1 : 2 * QUAD - 2]
    far, (attended_ref, keyval_ref, q_ref, out_ref) = refs[2 * QUAD - 2 : -4], refs[-4:]
    cut = own_ref.shape[1]
    chunks = cut // LANES
    slots = key_ref.shape[1]
    fold = 2 * BLOCK
    parts = [stats_ref[...]] + [unpack_stats(r[:, cut:]) for r in late]
    merged, near_shifts = merge_stats(parts)
    packed = [pack_side(side_ref[...])]
    packed += [r[:fold, cut + LANES :].astype(jnp.float32) for r in early]
    parts = [merged] + [unpack_stats(r[:, cut : cut + LANES]) for r in far]
    merged, far_shifts = merge_stats(parts)
    packed += [summed_ref[...]] + [r[:, cut + LANES :].astype(jnp.float32) for r in far]
    shifts = near_shifts + far_shifts
    mean, square = merged[:, 0:1], merged[:, 1:2]
    scale = lax.rsqrt(square - mean * mean + EPSILON)
    cosine, sine = cos_ref[...], sin_ref[...]
    new_key = new_value = None
    for c in range(0, chunks, 2):
        pair = []
        for d in (c, c + 1):
            columns = slice(d * LANES, (d + 1) * LANES)
            total = own_ref[:, columns]
            for r in (*late, *far):
                total = total + r[:, columns].astype(jnp.float32)
            for shift, side in zip(shifts, packed):
                total = total + shift * folded_row(side, d)
            pair.append(total * scale)
        for half in range(2):
            u1, u2 = (v[half * BLOCK : (half + 1) * BLOCK] for v in pair)
            number = half * (chunks // 2) + c // 2 - 2
            if number == -1:
                new_value = jnp.concatenate([u1, u2], axis=1)
                continue
            turned = (u1 * cosine - u2 * sine, u2 * cosine + u1 * sine)
            if number == -2:
                new_key = jnp.concatenate(turned, axis=1)
            else:
                for k in range(2):
                    q_ref[k, number * BLOCK : (number + 1) * BLOCK, :] = turned[k]
    keyval_ref[:, :HD] = new_key
    keyval_ref[:, HD:] = new_value
    factor = 1.0 / math.sqrt(HD)
    slot = lax.broadcasted_iota(jnp.int32, (heads, slots), 1)
    key_rounded = new_key.astype(jnp.bfloat16).astype(jnp.float32)
    value_rounded = new_value.astype(jnp.bfloat16).astype(jnp.float32)
    requests = range(BLOCK)
    queries = [
        jnp.concatenate(
            [q_ref.at[k][pl.ds(r, heads, stride=BLOCK), :] for k in range(2)], axis=1
        )
        for r in requests
    ]
    scores = [
        two_part_dot(queries[r], key_ref[r], (((1,), (1,)), ((), ()))) for r in requests
    ]
    own_scores = [
        jnp.sum(queries[r] * key_rounded[r : r + 1], axis=1, keepdims=True)
        * factor
        for r in requests
    ]
    masked = [jnp.where(slot < length_ref[r], scores[r] * factor, -jnp.inf) for r in requests]
    highest = [
        jnp.maximum(jnp.max(masked[r], axis=1, keepdims=True), own_scores[r]) for r in requests
    ]
    exps = [jnp.exp(masked[r] - highest[r]) for r in requests]
    own_exps = [jnp.exp(own_scores[r] - highest[r]) for r in requests]
    inverse = [
        1.0 / (jnp.sum(exps[r], axis=1, keepdims=True) + own_exps[r]) for r in requests
    ]
    mixed = [
        two_part_dot(exps[r], value_ref[r], (((1,), (0,)), ((), ()))) * inverse[r] for r in requests
    ]
    for r in requests:
        own_weight = own_exps[r] * inverse[r]
        result = mixed[r] + own_weight * value_rounded[r : r + 1]
        for k in range(2):
            out_ref.at[k][pl.ds(r, heads, stride=BLOCK), :] = result[:, k * LANES : (k + 1) * LANES]
    for h in range(heads // 2):
        upper_head = h + heads // 2
        for k in range(2):
            at = h * HD + k * LANES
            attended_ref[:, at : at + LANES] = jnp.concatenate(
                [out_ref[k, g * BLOCK : (g + 1) * BLOCK, :] for g in (h, upper_head)], axis=0
            ).astype(jnp.bfloat16)


def attend(lengths, after, own, stats, side, summed, tables, key_cache, value_cache, early, late, far,
           heads):
    return pl.pallas_call(
        functools.partial(attend_kernel, heads),
        in_specs=[SMEM, pl.BlockSpec(memory_space=pl.ANY)]
        + [VMEM] * (8 + len(early) + len(late) + len(far)),
        out_specs=[VMEM] * 2,
        out_shape=[
            struct((2 * BLOCK, heads * HD // 2), jnp.bfloat16),
            struct((BLOCK, 2 * HD), jnp.float32),
        ],
        scratch_shapes=[
            pltpu.VMEM((2, heads * BLOCK, LANES), jnp.float32),
            pltpu.VMEM((2, heads * BLOCK, LANES), jnp.float32),
        ],
        compiler_params=pltpu.CompilerParams(vmem_limit_bytes=24 * 2**20),
        name="attend",
    )(
        lengths, after, own, stats, side, summed, *tables, key_cache, value_cache, *early, *late, *far
    )


def load_kernel(base, w_hbm, after_ref, out_ref, token_ref, sems):
    parts = sems.shape[0]
    rows = out_ref.shape[0] // parts
    copies = [
        pltpu.make_async_copy(
            w_hbm.at[base + k * rows : base + (k + 1) * rows, :],
            out_ref.at[k * rows : (k + 1) * rows, :],
            sems.at[k],
        )
        for k in range(parts)
    ]
    for copy in copies:
        copy.start()
    for copy in copies:
        copy.wait()
    token_ref[...] = jnp.zeros_like(token_ref)


def load(begin, end, w_output, after):
    return pl.pallas_call(
        functools.partial(load_kernel, begin),
        in_specs=[pl.BlockSpec(memory_space=pltpu.HBM), pl.BlockSpec(memory_space=pl.ANY)],
        out_specs=[VMEM] * 2,
        out_shape=[
            struct((end - begin, w_output.shape[1]), w_output.dtype),
            struct((BLOCK, LANES), jnp.float32),
        ],
        scratch_shapes=[pltpu.SemaphoreType.DMA((PARTS,))],
        compiler_params=pltpu.CompilerParams(vmem_limit_bytes=16 * 2**20),
        cost_estimate=pl.CostEstimate(
            flops=0, bytes_accessed=2 * (end - begin) * w_output.shape[1], transcendentals=0
        ),
        name="load",
    )(in_hbm(w_output), after)


def unfold(lhs_ref, pieces):
    cut = pieces[0].shape[1]
    for k in range(0, len(pieces), 2):
        pair = [p.astype(jnp.float32) for p in pieces[k : k + 2]]
        at = slice(k * BLOCK, (k + 2) * BLOCK)
        lhs_ref[at, :cut] = jnp.concatenate([p[:BLOCK] for p in pair], axis=0).astype(jnp.bfloat16)
        lhs_ref[at, cut:] = jnp.concatenate([p[BLOCK:] for p in pair], axis=0).astype(jnp.bfloat16)


def unfold_kernel(*refs):
    fold = 2 * BLOCK
    unfold(
        refs[-1],
        [r[k : k + fold, :] for r in refs[:-1] for k in range(0, r.shape[0], fold)],
    )


def stack_kernel(*refs):
    at = 0
    for r in refs[:-1]:
        refs[-1][at : at + r.shape[0], :] = r[...]
        at += r.shape[0]


def stack(pieces):
    return pl.pallas_call(
        stack_kernel,
        in_specs=[VMEM] * len(pieces),
        out_specs=VMEM,
        out_shape=struct((sum(p.shape[0] for p in pieces), pieces[0].shape[1]), jnp.bfloat16),
        compiler_params=pltpu.CompilerParams(vmem_limit_bytes=16 * 2**20),
        name="stack",
    )(*pieces)


def unfold_rows(pieces):
    return pl.pallas_call(
        unfold_kernel,
        in_specs=[VMEM] * len(pieces),
        out_specs=VMEM,
        out_shape=struct(
            (sum(p.shape[0] for p in pieces) // 2, 2 * pieces[0].shape[1]), jnp.bfloat16
        ),
        compiler_params=pltpu.CompilerParams(vmem_limit_bytes=16 * 2**20),
        name="unfold_rows",
    )(*pieces)


def output_kernel(order, parts, me_ref, x_ref, *refs):
    weights, refs = refs[:parts], refs[parts:]
    pieces, (out_hbm, rows_ref, sum_ref, sems) = refs[:-4], refs[-4:]
    me = me_ref[0]
    width = x_ref.shape[1]
    rows_ref[...] = x_ref[...].astype(jnp.float32)
    copies = []
    for k, left in enumerate(range(0, width, TILE)):
        columns = slice(left, min(left + TILE, width))
        total = 0.0
        begin = 0
        for w in weights:
            end = begin + w.shape[0]
            total = total + jnp.dot(
                jnp.concatenate([p[:, begin:end] for p in pieces], axis=0),
                w[:, columns],
                preferred_element_type=jnp.float32,
            )
            begin = end
        sum_ref[:, columns] = total
        for p, b in enumerate(order):
            at = pl.ds(pl.multiple_of((me ^ b) * BLOCK, BLOCK), BLOCK)
            rows_ref[at, columns] = (
                rows_ref[at, columns] + sum_ref[p * BLOCK : (p + 1) * BLOCK, columns]
            )
        copies.append(
            pltpu.make_async_copy(rows_ref.at[:, columns], out_hbm.at[:, columns], sems.at[k])
        )
        copies[-1].start()
    for copy in copies:
        copy.wait()


def output(me, order, pieces, residual, weights):
    total, width = residual.shape
    return pl.pallas_call(
        functools.partial(output_kernel, order, len(weights)),
        in_specs=[SMEM] + [VMEM] * (1 + len(weights) + len(pieces)),
        out_specs=pl.BlockSpec(memory_space=pltpu.HBM),
        out_shape=struct((total, width), jnp.float32),
        scratch_shapes=[
            pltpu.VMEM((total, width), jnp.float32),
            pltpu.VMEM((total, width), jnp.float32),
            pltpu.SemaphoreType.DMA((-(-width // TILE),)),
        ],
        compiler_params=pltpu.CompilerParams(vmem_limit_bytes=24 * 2**20),
        name="output",
    )(me, residual, *weights, *pieces)


def local(
    residual, norm_gain, w_query, w_keyval, w_output, key_cache, value_cache, lengths, positions
):
    count = lax.axis_size("gx")
    me = lax.axis_index("gx").astype(jnp.int32).reshape(1)
    heads = w_query.shape[1] // HD
    groups = count // (2 * QUAD)
    quad_masks = [2 * q for q in range(1, QUAD)]
    far_masks = [2 * QUAD * g for g in range(1, groups)]
    order = [
        core + 2 * q + 2 * QUAD * g for core in range(2) for g in range(groups) for q in range(QUAD)
    ]
    tables = rope_tables(positions)

    keep, send, stats, extra = project(me, order, residual, norm_gain, w_query, w_keyval)
    recv = exchange(send, 1, count)
    other = exchange(extra, 1, count)
    own, far, own_stats, far_stats, side, *sends = first_combine(keep, recv, stats, extra, other)
    early = [exchange(v, m, count) for v, m in zip(sends[: QUAD - 1], quad_masks)]
    far = far_add(far, early[-1])
    summed, *far_sends = far_combine(far, far_stats, side, early)
    late = [exchange(v, m, count) for v, m in zip(sends[QUAD - 1 :], quad_masks)]
    depth = w_output.shape[0]
    cuts = [0] + [depth * part // 16 for part in LOADS]
    first, token = load(cuts[0], cuts[1], w_output, summed)
    far_sums = [exchange(v, m, count) for v, m in zip(far_sends, far_masks)]
    attended, new_keyval = attend(
        lengths, token, own, own_stats, side, summed, tables, key_cache, value_cache, early, late,
        far_sums, heads,
    )

    near_masks, diagonal_mask = quad_masks[:-1], quad_masks[-1]
    far_own = [exchange(attended, m, count) for m in far_masks]
    near_pieces = [attended] + [exchange(attended, m, count) for m in near_masks] + far_own
    far_pieces = [exchange(piece, mask, count) for piece in far_own for mask in near_masks]
    far_pieces += [exchange(p, diagonal_mask, count) for p in [attended] + far_own]
    near_order = [[core + b for b in [0] + near_masks + far_masks] for core in range(2)]
    far_order = [
        [core + b for b in [far + near for far in far_masks for near in near_masks]
         + [far + diagonal_mask for far in [0] + far_masks]]
        for core in range(2)
    ]
    second, token = load(cuts[1], cuts[2], w_output, far_own[0])
    near_rows = unfold_rows([behind(p, token) for p in near_pieces])
    far_rows = unfold_rows([behind(p, token) for p in far_pieces])
    updated = output(
        me,
        near_order[0] + near_order[1] + far_order[0] + far_order[1],
        [near_rows, exchange(near_rows, 1, count), far_rows, exchange(far_rows, 1, count)],
        residual,
        (first, second),
    )
    return (updated, new_keyval)


def solution(mesh):
    in_specs = (
        P("groups", "gx"),
        P("gx"),
        P("gx", None),
        P("gx", None),
        P(None, "gx"),
        P(("groups", "gx"), None, None),
        P(("groups", "gx"), None, None),
        P(("groups", "gx")),
        P(("groups", "gx")),
    )
    out_specs = (P("groups", "gx"), P(("groups", "gx"), None))
    return jax.shard_map(local, mesh=mesh, in_specs=in_specs, out_specs=out_specs, check_vma=False)
```

```python
import functools
import math

import jax
import jax.numpy as jnp
from jax import lax
from jax.experimental import pallas as pl
from jax.experimental.pallas import tpu as pltpu
from jax.sharding import PartitionSpec as P

HD = 256
LANES = 128
BLOCK = 8
TILE = 512
WIDE = 1024
SIDE = 32
AHEAD = 3
PACE = 1
QUAD = 4
PARTS = 4
LOADS = (11, 16)
EPSILON = 1e-05
VMEM = pl.BlockSpec(memory_space=pltpu.VMEM)
SMEM = pl.BlockSpec(memory_space=pltpu.SMEM)


def rope_tables(position_rows):
    half_width = HD // 2
    inverse_freq = 10000.0 ** (-(jnp.arange(half_width, dtype=jnp.float32) * 2.0 / HD))
    angles = position_rows.astype(jnp.float32)[:, None] * inverse_freq[None, :]
    return (jnp.cos(angles), jnp.sin(angles))


def exchange(value, mask, count):
    return lax.ppermute(value, "gx", [(i, i ^ mask) for i in range(count)])


def behind(value, first):
    return lax.optimization_barrier((value, first))[0]


def in_hbm(value):
    return pltpu.with_memory_space_constraint(value, pltpu.HBM)


def struct(shape, dtype):
    return jax.ShapeDtypeStruct(shape, dtype)


def lane_ids(rows):
    return lax.broadcasted_iota(jnp.int32, (rows, LANES), 1)


def pack_stats(stats):
    high = stats.astype(jnp.bfloat16).astype(jnp.float32)
    middle = (stats - high).astype(jnp.bfloat16).astype(jnp.float32)
    low = stats - high - middle
    lane = lane_ids(stats.shape[0])
    return jnp.where(lane < 2, high, jnp.where(lane < 4, middle, low)).astype(jnp.bfloat16)


def unpack_stats(packed):
    parts = packed.astype(jnp.float32)
    mean = parts[:, 0:1] + parts[:, 2:3] + parts[:, 4:5]
    square = parts[:, 1:2] + parts[:, 3:4] + parts[:, 5:6]
    return jnp.where(lane_ids(parts.shape[0]) % 2 == 0, mean, square)


def pack_side(side):
    pieces = []
    for start in range(0, SIDE, BLOCK):
        pieces.append(
            jnp.concatenate(
                [side[start : start + BLOCK], side[SIDE + start : SIDE + start + BLOCK]], axis=0
            )
        )
    return jnp.concatenate(pieces, axis=1)


def folded_row(packed, c):
    part = packed[:, c // BLOCK * LANES : (c // BLOCK + 1) * LANES]
    k = c % BLOCK
    upper = lax.broadcasted_iota(jnp.int32, (2 * BLOCK, LANES), 0) >= BLOCK
    return jnp.where(upper, part[BLOCK + k : BLOCK + k + 1], part[k : k + 1])


def merge_stats(parts):
    merged = sum(parts[1:], parts[0]) * (1.0 / len(parts))
    return merged, [p[:, 0:1] - merged[:, 0:1] for p in parts]


def project_kernel(order, me_ref, x_hbm, gain_hbm, wq_hbm, wkv_hbm, keep_ref, send_ref, stats_ref,
                   extra_ref, x_ref, gain_ref, rows_ref, lhs_ref, wkv_ref, w_ref, in_sem,
                   w_sem):
    total = x_ref.shape[0]
    half = total // 2
    me = me_ref[0]
    tiles = w_sem.shape[0]
    x_copy = pltpu.make_async_copy(x_hbm, x_ref, in_sem.at[0])
    gain_copy = pltpu.make_async_copy(gain_hbm, gain_ref, in_sem.at[1])
    x_copy.start()
    gain_copy.start()
    copies = []
    for t in range(tiles):
        if t == 0:
            source, target = wkv_hbm, wkv_ref
        else:
            source, target = wq_hbm.at[:, (t - 1) * WIDE : t * WIDE], w_ref.at[t - 1]
        copies.append(pltpu.make_async_copy(source, target, w_sem.at[t]))
    started = min(AHEAD, tiles)
    for t in range(started):
        copies[t].start()
    x_copy.wait()
    gain_copy.wait()
    rows_ref[...] = x_ref[...].astype(jnp.float32)
    gain = gain_ref[...].reshape(1, gain_ref.shape[0])
    high = gain.astype(jnp.bfloat16).astype(jnp.float32)
    low = gain - high
    row = lax.broadcasted_iota(jnp.int32, (16, gain.shape[1]), 0)
    lhs_ref[total:, :] = jnp.where(
        row == 0, high, jnp.where(row == 1, low, 0.0)
    ).astype(jnp.bfloat16)
    lane = lane_ids(2 * BLOCK)
    extra_ref[half:, :] = jnp.zeros((2 * SIDE, LANES), jnp.float32)
    for pair in range(len(order) // 2):
        pieces = []
        for b in order[2 * pair : 2 * pair + 2]:
            start = pl.multiple_of((me ^ b) * BLOCK, BLOCK)
            pieces.append(rows_ref[pl.ds(start, BLOCK), :])
        x = jnp.concatenate(pieces, axis=0)
        mean = jnp.mean(x, axis=1, keepdims=True)
        square = jnp.mean(x * x, axis=1, keepdims=True)
        at = pair * 2 * BLOCK
        lhs_ref[at : at + 2 * BLOCK, :] = ((x - mean) * gain).astype(jnp.bfloat16)
        if started < tiles - 1 and pair % PACE == PACE - 1:
            copies[started].start()
            started += 1
        stats = jnp.where(lane % 2 == 0, mean, square)
        if at < half:
            stats_ref[at : at + 2 * BLOCK, :] = stats
        else:
            extra_ref[at - half : at - half + 2 * BLOCK, :] = stats

    chunks = keep_ref.shape[1] // LANES // 2
    at_column = 0
    for t in range(tiles):
        while started < min(tiles, t + AHEAD + 4):
            copies[started].start()
            started += 1
        copies[t].wait()
        weights = wkv_ref if t == 0 else w_ref.at[t - 1]
        for start in range(0, weights.shape[1], TILE):
            out = jnp.dot(
                lhs_ref[...], weights[:, start : start + TILE], preferred_element_type=jnp.float32
            )
            columns = slice(at_column, at_column + TILE)
            keep_ref[:, columns] = out[:half]
            send_ref[:, columns] = out[half:total].astype(jnp.bfloat16)
            gained = out[total : total + 1] + out[total + 1 : total + 2]
            for k in range(TILE // LANES):
                c = at_column // LANES + k
                at = half + c if c < chunks else half + SIDE + c - chunks
                extra_ref[at : at + 1, :] = gained[:, k * LANES : (k + 1) * LANES]
            at_column += TILE


def project(me, order, residual, gain, w_query, w_keyval):
    total, depth = residual.shape
    width = w_query.shape[1] + w_keyval.shape[1]
    half = total // 2
    return pl.pallas_call(
        functools.partial(project_kernel, order),
        in_specs=[SMEM] + [pl.BlockSpec(memory_space=pltpu.HBM)] * 4,
        out_specs=[VMEM] * 4,
        out_shape=[
            struct((half, width), jnp.float32),
            struct((half, width), jnp.bfloat16),
            struct((half, LANES), jnp.float32),
            struct((half + 2 * SIDE, LANES), jnp.float32),
        ],
        scratch_shapes=[
            pltpu.VMEM((total, depth), jnp.bfloat16),
            pltpu.VMEM((depth,), jnp.float32),
            pltpu.VMEM((total, depth), jnp.float32),
            pltpu.VMEM((total + 16, depth), jnp.bfloat16),
            pltpu.VMEM((depth, w_keyval.shape[1]), jnp.bfloat16),
            pltpu.VMEM((w_query.shape[1] // WIDE, depth, WIDE), jnp.bfloat16),
            pltpu.SemaphoreType.DMA((2,)),
            pltpu.SemaphoreType.DMA((1 + w_query.shape[1] // WIDE,)),
        ],
        compiler_params=pltpu.CompilerParams(vmem_limit_bytes=24 * 2**20),
        name="project",
    )(me, *(in_hbm(v) for v in (residual, gain, w_query, w_keyval)))


def first_kernel(keep_ref, recv_ref, stats_ref, extra_ref, other_ref,
                 own_ref, far_ref, own_stats, far_stats, side_ref, *send_refs):
    half, width = keep_ref.shape
    cut = width // 2
    chunks = cut // LANES
    early, late = send_refs[: QUAD - 1], send_refs[QUAD - 1 :]
    own = stats_ref[...]
    other = other_ref[:half, :]
    merged = 0.5 * (own + other)
    shift = 0.5 * (own[:, 0:1] - other[:, 0:1])
    side = extra_ref[half:, :] + other_ref[half:, :]
    change = extra_ref[half:, :] - other_ref[half:, :]
    side_ref[...] = side
    packed_side = pack_side(side).astype(jnp.bfloat16)
    fold = 2 * BLOCK

    def target(k):
        group, q = divmod(k, QUAD)
        return group, q, slice((group - 1) * fold, group * fold)

    for k in range(half // BLOCK):
        group, q, at = target(k)
        stats = merged[k * BLOCK : (k + 1) * BLOCK]
        stats = jnp.concatenate([stats, stats], axis=0)
        if q == 0:
            if group == 0:
                own_stats[...] = stats
            else:
                far_stats[at, :] = stats
        elif group == 0:
            late[q - 1][:, cut:] = pack_stats(stats)
        else:
            early[q - 1][at, cut : cut + LANES] = pack_stats(stats)
            early[q - 1][at, cut + LANES :] = packed_side
    for c in range(chunks):
        columns = slice(c * LANES, (c + 1) * LANES)
        totals = []
        for n in range(2):
            source = slice(n * cut + c * LANES, n * cut + (c + 1) * LANES)
            row = n * SIDE + c
            totals.append(
                keep_ref[:, source]
                + recv_ref[:, source].astype(jnp.float32)
                + shift * change[row : row + 1]
            )
        for k in range(half // BLOCK):
            group, q, at = target(k)
            value = jnp.concatenate([t[k * BLOCK : (k + 1) * BLOCK] for t in totals], axis=0)
            if q == 0:
                if group == 0:
                    own_ref[:, columns] = value
                else:
                    far_ref[at, columns] = value
            elif group == 0:
                late[q - 1][:, columns] = value.astype(jnp.bfloat16)
            else:
                early[q - 1][at, columns] = value.astype(jnp.bfloat16)


def first_combine(keep, recv, stats, extra, other):
    half, width = keep.shape
    cut = width // 2
    fold = 2 * BLOCK
    groups = half // (QUAD * BLOCK)
    far = (groups - 1) * fold
    return pl.pallas_call(
        first_kernel,
        in_specs=[VMEM] * 5,
        out_specs=[VMEM] * (5 + 2 * (QUAD - 1)),
        out_shape=[
            struct((fold, cut), jnp.float32),
            struct((far, cut), jnp.float32),
            struct((fold, LANES), jnp.float32),
            struct((far, LANES), jnp.float32),
            struct((2 * SIDE, LANES), jnp.float32),
        ]
        + [struct((far, cut + LANES + SIDE // BLOCK * LANES), jnp.bfloat16)] * (QUAD - 1)
        + [struct((fold, cut + LANES), jnp.bfloat16)] * (QUAD - 1),
        compiler_params=pltpu.CompilerParams(vmem_limit_bytes=16 * 2**20),
        name="first_combine",
    )(keep, recv, stats, extra, other)


def far_add_kernel(far_ref, recv_ref, out_ref):
    cut = far_ref.shape[1]
    out_ref[...] = far_ref[...] + recv_ref[:, :cut].astype(jnp.float32)


def far_add(far, recv):
    return pl.pallas_call(
        far_add_kernel,
        in_specs=[VMEM] * 2,
        out_specs=VMEM,
        out_shape=struct(far.shape, far.dtype),
        compiler_params=pltpu.CompilerParams(vmem_limit_bytes=16 * 2**20),
        name="far_add",
    )(far, recv)


def far_kernel(far_ref, stats_ref, side_ref, *refs):
    recv, outs = refs[: QUAD - 1], refs[QUAD - 1 :]
    cut = far_ref.shape[1]
    fold = 2 * BLOCK
    packed = [r[:fold, cut + LANES :].astype(jnp.float32) for r in recv]
    packed = [pack_side(side_ref[...])] + packed
    summed = sum(packed[1:], packed[0])
    outs[0][...] = summed
    for g, out in enumerate(outs[1:]):
        at = slice(g * fold, (g + 1) * fold)
        parts = [stats_ref[at, :]] + [unpack_stats(r[at, cut : cut + LANES]) for r in recv]
        merged, shifts = merge_stats(parts)
        out[:, cut : cut + LANES] = pack_stats(merged)
        out[:, cut + LANES :] = summed.astype(jnp.bfloat16)
        for c in range(cut // LANES):
            columns = slice(c * LANES, (c + 1) * LANES)
            total = far_ref[at, columns]
            for r in recv[:-1]:
                total = total + r[at, columns].astype(jnp.float32)
            for shift, side in zip(shifts, packed):
                total = total + shift * folded_row(side, c)
            out[:, columns] = total.astype(jnp.bfloat16)


def far_combine(far, stats, side, recv):
    cut = far.shape[1]
    fold = 2 * BLOCK
    groups = far.shape[0] // fold
    side_columns = SIDE // BLOCK * LANES
    return pl.pallas_call(
        far_kernel,
        in_specs=[VMEM] * (3 + QUAD - 1),
        out_specs=[VMEM] * (1 + groups),
        out_shape=[struct((fold, side_columns), jnp.float32)]
        + [struct((fold, cut + LANES + side_columns), jnp.bfloat16)] * groups,
        compiler_params=pltpu.CompilerParams(vmem_limit_bytes=16 * 2**20),
        name="far_combine",
    )(far, stats, side, *recv)


def two_part_dot(left, right, dims):
    rows = left.shape[0]
    high = left.astype(jnp.bfloat16)
    low = (left - high.astype(jnp.float32)).astype(jnp.bfloat16)
    both = jnp.concatenate([high.astype(jnp.float32), low.astype(jnp.float32)], axis=0)
    out = lax.dot_general(
        both.astype(jnp.bfloat16), right, dims, preferred_element_type=jnp.float32
    )
    return out[:rows] + out[rows:]


def attend_kernel(heads, length_ref, after_ref, own_ref, stats_ref, side_ref, summed_ref, cos_ref, sin_ref,
                  key_ref, value_ref, *refs):
    early, late = refs[: QUAD - 1], refs[QUAD - 1 : 2 * QUAD - 2]
    far, (attended_ref, keyval_ref, q_ref, out_ref) = refs[2 * QUAD - 2 : -4], refs[-4:]
    cut = own_ref.shape[1]
    chunks = cut // LANES
    slots = key_ref.shape[1]
    fold = 2 * BLOCK
    parts = [stats_ref[...]] + [unpack_stats(r[:, cut:]) for r in late]
    merged, near_shifts = merge_stats(parts)
    packed = [pack_side(side_ref[...])]
    packed += [r[:fold, cut + LANES :].astype(jnp.float32) for r in early]
    parts = [merged] + [unpack_stats(r[:, cut : cut + LANES]) for r in far]
    merged, far_shifts = merge_stats(parts)
    packed += [summed_ref[...]] + [r[:, cut + LANES :].astype(jnp.float32) for r in far]
    shifts = near_shifts + far_shifts
    mean, square = merged[:, 0:1], merged[:, 1:2]
    scale = lax.rsqrt(square - mean * mean + EPSILON)
    cosine, sine = cos_ref[...], sin_ref[...]
    new_key = new_value = None
    for c in range(0, chunks, 2):
        pair = []
        for d in (c, c + 1):
            columns = slice(d * LANES, (d + 1) * LANES)
            total = own_ref[:, columns]
            for r in (*late, *far):
                total = total + r[:, columns].astype(jnp.float32)
            for shift, side in zip(shifts, packed):
                total = total + shift * folded_row(side, d)
            pair.append(total * scale)
        for half in range(2):
            u1, u2 = (v[half * BLOCK : (half + 1) * BLOCK] for v in pair)
            number = half * (chunks // 2) + c // 2 - 2
            if number == -1:
                new_value = jnp.concatenate([u1, u2], axis=1)
                continue
            turned = (u1 * cosine - u2 * sine, u2 * cosine + u1 * sine)
            if number == -2:
                new_key = jnp.concatenate(turned, axis=1)
            else:
                for k in range(2):
                    q_ref[k, number * BLOCK : (number + 1) * BLOCK, :] = turned[k]
    keyval_ref[:, :HD] = new_key
    keyval_ref[:, HD:] = new_value
    factor = 1.0 / math.sqrt(HD)
    slot = lax.broadcasted_iota(jnp.int32, (heads, slots), 1)
    key_rounded = new_key.astype(jnp.bfloat16).astype(jnp.float32)
    value_rounded = new_value.astype(jnp.bfloat16).astype(jnp.float32)
    requests = range(BLOCK)
    queries = [
        jnp.concatenate(
            [q_ref.at[k][pl.ds(r, heads, stride=BLOCK), :] for k in range(2)], axis=1
        )
        for r in requests
    ]
    scores = [
        two_part_dot(queries[r], key_ref[r], (((1,), (1,)), ((), ()))) for r in requests
    ]
    own_scores = [
        jnp.sum(queries[r] * key_rounded[r : r + 1], axis=1, keepdims=True)
        * factor
        for r in requests
    ]
    masked = [jnp.where(slot < length_ref[r : r + 1, 0:1], scores[r] * factor, -jnp.inf) for r in requests]
    highest = [
        jnp.maximum(jnp.max(masked[r], axis=1, keepdims=True), own_scores[r]) for r in requests
    ]
    exps = [jnp.exp(masked[r] - highest[r]) for r in requests]
    own_exps = [jnp.exp(own_scores[r] - highest[r]) for r in requests]
    inverse = [
        1.0 / (jnp.sum(exps[r], axis=1, keepdims=True) + own_exps[r]) for r in requests
    ]
    mixed = [
        two_part_dot(exps[r], value_ref[r], (((1,), (0,)), ((), ()))) * inverse[r] for r in requests
    ]
    for r in requests:
        own_weight = own_exps[r] * inverse[r]
        result = mixed[r] + own_weight * value_rounded[r : r + 1]
        for k in range(2):
            out_ref.at[k][pl.ds(r, heads, stride=BLOCK), :] = result[:, k * LANES : (k + 1) * LANES]
    for h in range(heads // 2):
        upper_head = h + heads // 2
        for k in range(2):
            at = h * HD + k * LANES
            attended_ref[:, at : at + LANES] = jnp.concatenate(
                [out_ref[k, g * BLOCK : (g + 1) * BLOCK, :] for g in (h, upper_head)], axis=0
            ).astype(jnp.bfloat16)


def attend(lengths, after, own, stats, side, summed, tables, key_cache, value_cache, early, late, far,
           heads):
    return pl.pallas_call(
        functools.partial(attend_kernel, heads),
        in_specs=[VMEM, pl.BlockSpec(memory_space=pl.ANY)]
        + [VMEM] * (8 + len(early) + len(late) + len(far)),
        out_specs=[VMEM] * 2,
        out_shape=[
            struct((2 * BLOCK, heads * HD // 2), jnp.bfloat16),
            pltpu.VMEM((BLOCK, 2 * HD), jnp.float32),
        ],
        scratch_shapes=[
            pltpu.VMEM((2, heads * BLOCK, LANES), jnp.float32),
            pltpu.VMEM((2, heads * BLOCK, LANES), jnp.float32),
        ],
        compiler_params=pltpu.CompilerParams(vmem_limit_bytes=24 * 2**20),
        name="attend",
    )(
        lengths, after, own, stats, side, summed, *tables, key_cache, value_cache, *early, *late, *far
    )


def load_and_write_kernel(base, w_hbm, after_ref, value_ref, out_ref, token_ref, value_hbm, sems,
                          value_sem):
    write = pltpu.make_async_copy(value_ref, value_hbm, value_sem)
    write.start()
    load_kernel(base, w_hbm, after_ref, out_ref, token_ref, sems)
    write.wait()


def load_and_write(begin, end, w_output, after, value):
    return pl.pallas_call(
        functools.partial(load_and_write_kernel, begin),
        in_specs=[
            pl.BlockSpec(memory_space=pltpu.HBM),
            pl.BlockSpec(memory_space=pl.ANY),
            VMEM,
        ],
        out_specs=[VMEM] * 2 + [pl.BlockSpec(memory_space=pltpu.HBM)],
        out_shape=[
            struct((end - begin, w_output.shape[1]), w_output.dtype),
            struct((BLOCK, LANES), jnp.float32),
            struct(value.shape, value.dtype),
        ],
        scratch_shapes=[pltpu.SemaphoreType.DMA((PARTS,)), pltpu.SemaphoreType.DMA],
        compiler_params=pltpu.CompilerParams(vmem_limit_bytes=16 * 2**20),
        cost_estimate=pl.CostEstimate(
            flops=0, bytes_accessed=2 * (end - begin) * w_output.shape[1], transcendentals=0
        ),
        name="load_and_write",
    )(in_hbm(w_output), after, value)


def load_kernel(base, w_hbm, after_ref, out_ref, token_ref, sems):
    parts = sems.shape[0]
    rows = out_ref.shape[0] // parts
    copies = [
        pltpu.make_async_copy(
            w_hbm.at[base + k * rows : base + (k + 1) * rows, :],
            out_ref.at[k * rows : (k + 1) * rows, :],
            sems.at[k],
        )
        for k in range(parts)
    ]
    for copy in copies:
        copy.start()
    for copy in copies:
        copy.wait()
    token_ref[...] = jnp.zeros_like(token_ref)


def load(begin, end, w_output, after):
    return pl.pallas_call(
        functools.partial(load_kernel, begin),
        in_specs=[pl.BlockSpec(memory_space=pltpu.HBM), pl.BlockSpec(memory_space=pl.ANY)],
        out_specs=[VMEM] * 2,
        out_shape=[
            struct((end - begin, w_output.shape[1]), w_output.dtype),
            struct((BLOCK, LANES), jnp.float32),
        ],
        scratch_shapes=[pltpu.SemaphoreType.DMA((PARTS,))],
        compiler_params=pltpu.CompilerParams(vmem_limit_bytes=16 * 2**20),
        cost_estimate=pl.CostEstimate(
            flops=0, bytes_accessed=2 * (end - begin) * w_output.shape[1], transcendentals=0
        ),
        name="load",
    )(in_hbm(w_output), after)


def unfold(lhs_ref, pieces):
    cut = pieces[0].shape[1]
    for k in range(0, len(pieces), 2):
        pair = [p.astype(jnp.float32) for p in pieces[k : k + 2]]
        at = slice(k * BLOCK, (k + 2) * BLOCK)
        lhs_ref[at, :cut] = jnp.concatenate([p[:BLOCK] for p in pair], axis=0).astype(jnp.bfloat16)
        lhs_ref[at, cut:] = jnp.concatenate([p[BLOCK:] for p in pair], axis=0).astype(jnp.bfloat16)


def unfold_kernel(*refs):
    fold = 2 * BLOCK
    unfold(
        refs[-1],
        [r[k : k + fold, :] for r in refs[:-1] for k in range(0, r.shape[0], fold)],
    )


def stack_kernel(*refs):
    at = 0
    for r in refs[:-1]:
        refs[-1][at : at + r.shape[0], :] = r[...]
        at += r.shape[0]


def stack(pieces):
    return pl.pallas_call(
        stack_kernel,
        in_specs=[VMEM] * len(pieces),
        out_specs=VMEM,
        out_shape=struct((sum(p.shape[0] for p in pieces), pieces[0].shape[1]), jnp.bfloat16),
        compiler_params=pltpu.CompilerParams(vmem_limit_bytes=16 * 2**20),
        name="stack",
    )(*pieces)


def unfold_rows(pieces):
    return pl.pallas_call(
        unfold_kernel,
        in_specs=[VMEM] * len(pieces),
        out_specs=VMEM,
        out_shape=struct(
            (sum(p.shape[0] for p in pieces) // 2, 2 * pieces[0].shape[1]), jnp.bfloat16
        ),
        compiler_params=pltpu.CompilerParams(vmem_limit_bytes=16 * 2**20),
        name="unfold_rows",
    )(*pieces)


def output_kernel(order, parts, me_ref, x_ref, *refs):
    weights, refs = refs[:parts], refs[parts:]
    pieces, (out_hbm, rows_ref, sum_ref, sems) = refs[:-4], refs[-4:]
    me = me_ref[0]
    width = x_ref.shape[1]
    rows_ref[...] = x_ref[...].astype(jnp.float32)
    copies = []
    for k, left in enumerate(range(0, width, TILE)):
        columns = slice(left, min(left + TILE, width))
        total = 0.0
        begin = 0
        for w in weights:
            end = begin + w.shape[0]
            total = total + jnp.dot(
                jnp.concatenate([p[:, begin:end] for p in pieces], axis=0),
                w[:, columns],
                preferred_element_type=jnp.float32,
            )
            begin = end
        sum_ref[:, columns] = total
        for p, b in enumerate(order):
            at = pl.ds(pl.multiple_of((me ^ b) * BLOCK, BLOCK), BLOCK)
            rows_ref[at, columns] = (
                rows_ref[at, columns] + sum_ref[p * BLOCK : (p + 1) * BLOCK, columns]
            )
        copies.append(
            pltpu.make_async_copy(rows_ref.at[:, columns], out_hbm.at[:, columns], sems.at[k])
        )
        copies[-1].start()
    for copy in copies:
        copy.wait()


def output(me, order, pieces, residual, weights):
    total, width = residual.shape
    return pl.pallas_call(
        functools.partial(output_kernel, order, len(weights)),
        in_specs=[SMEM] + [VMEM] * (1 + len(weights) + len(pieces)),
        out_specs=pl.BlockSpec(memory_space=pltpu.HBM),
        out_shape=struct((total, width), jnp.float32),
        scratch_shapes=[
            pltpu.VMEM((total, width), jnp.float32),
            pltpu.VMEM((total, width), jnp.float32),
            pltpu.SemaphoreType.DMA((-(-width // TILE),)),
        ],
        compiler_params=pltpu.CompilerParams(vmem_limit_bytes=24 * 2**20),
        name="output",
    )(me, residual, *weights, *pieces)


def local(
    residual, norm_gain, w_query, w_keyval, w_output, key_cache, value_cache, lengths, positions
):
    count = lax.axis_size("gx")
    me = lax.axis_index("gx").astype(jnp.int32).reshape(1)
    heads = w_query.shape[1] // HD
    groups = count // (2 * QUAD)
    quad_masks = [2 * q for q in range(1, QUAD)]
    far_masks = [2 * QUAD * g for g in range(1, groups)]
    order = [
        core + 2 * q + 2 * QUAD * g for core in range(2) for g in range(groups) for q in range(QUAD)
    ]
    tables = rope_tables(positions)
    limits = jnp.broadcast_to(lengths[:, None], (lengths.shape[0], LANES))

    keep, send, stats, extra = project(me, order, residual, norm_gain, w_query, w_keyval)
    recv = exchange(send, 1, count)
    other = exchange(extra, 1, count)
    own, far, own_stats, far_stats, side, *sends = first_combine(keep, recv, stats, extra, other)
    early = [exchange(v, m, count) for v, m in zip(sends[: QUAD - 1], quad_masks)]
    far = far_add(far, early[-1])
    summed, *far_sends = far_combine(far, far_stats, side, early)
    late = [exchange(v, m, count) for v, m in zip(sends[QUAD - 1 :], quad_masks)]
    depth = w_output.shape[0]
    cuts = [0] + [depth * part // 16 for part in LOADS]
    first, token = load(cuts[0], cuts[1], w_output, summed)
    far_sums = [exchange(v, m, count) for v, m in zip(far_sends, far_masks)]
    attended, new_keyval = attend(
        limits, token, own, own_stats, side, summed, tables, key_cache, value_cache, early, late,
        far_sums, heads,
    )

    near_masks, diagonal_mask = quad_masks[:-1], quad_masks[-1]
    far_own = [exchange(attended, m, count) for m in far_masks]
    near_pieces = [attended] + [exchange(attended, m, count) for m in near_masks] + far_own
    far_pieces = [exchange(piece, mask, count) for piece in far_own for mask in near_masks]
    far_pieces += [exchange(p, diagonal_mask, count) for p in [attended] + far_own]
    near_order = [[core + b for b in [0] + near_masks + far_masks] for core in range(2)]
    far_order = [
        [core + b for b in [far + near for far in far_masks for near in near_masks]
         + [far + diagonal_mask for far in [0] + far_masks]]
        for core in range(2)
    ]
    second, token, new_keyval = load_and_write(
        cuts[1], cuts[2], w_output, far_own[0], new_keyval
    )
    near_rows = unfold_rows([behind(p, token) for p in near_pieces])
    far_rows = unfold_rows([behind(p, token) for p in far_pieces])
    updated = output(
        me,
        near_order[0] + near_order[1] + far_order[0] + far_order[1],
        [near_rows, exchange(near_rows, 1, count), far_rows, exchange(far_rows, 1, count)],
        residual,
        (first, second),
    )
    return (updated, new_keyval)


def solution(mesh):
    in_specs = (
        P("groups", "gx"),
        P("gx"),
        P("gx", None),
        P("gx", None),
        P(None, "gx"),
        P(("groups", "gx"), None, None),
        P(("groups", "gx"), None, None),
        P(("groups", "gx")),
        P(("groups", "gx")),
    )
    out_specs = (P("groups", "gx"), P(("groups", "gx"), None))
    return jax.shard_map(local, mesh=mesh, in_specs=in_specs, out_specs=out_specs, check_vma=False)
```
